32 devices in a mesh: section: 4 (over z), dp: 8 (over y, x, core).
Axes of the slice: x: 2, y: 2, z: 4, core: 2. Of those that a mesh axis runs over, the one named last changes fastest.
Arguments:
- residues: bfloat16 [16, 256, 640], P('dp'), may hold values from -6 to 6
- out_grad: bfloat16 [16, 256, 640], P('dp'), may hold values from -6 to 6
- key_lengths: int32 [16], P('dp'), may hold values from 128 to 256, as said below
- masked: int32 [16, 256], P('dp'), may hold values from 0 to 1, as said below
- attn_gain: bfloat16 [2, 640], P(None, 'dp'), may hold values from 0.099609375 to 1.8984375
- attn_shift: bfloat16 [2, 640], P(None, 'dp'), may hold values from -3 to 3
- qkv_weight: bfloat16 [2, 640, 1920], P(None, 'dp'), may hold values from -0.25 to 0.25
- query_bias: bfloat16 [2, 640], P(None, 'dp'), may hold values from -3 to 3
- value_bias: bfloat16 [2, 640], P(None, 'dp'), may hold values from -0.29882812 to 0.29882812
- out_weight: bfloat16 [2, 640, 640], P(None, 'dp'), may hold values from -2.5 to 2.5
- out_bias: bfloat16 [2, 640], P(None, 'dp'), may hold values from -3 to 3
- ffn_gain: bfloat16 [2, 640], P(None, 'dp'), may hold values from 0.099609375 to 1.8984375
- ffn_shift: bfloat16 [2, 640], P(None, 'dp'), may hold values from -3 to 3
- up_weight: bfloat16 [2, 640, 5120], P(None, 'dp'), may hold values from -0.25 to 0.25
- up_bias: bfloat16 [2, 5120], P(None, 'dp'), may hold values from -3 to 3
- down_weight: bfloat16 [2, 5120, 640], P(None, 'dp'), may hold values from -0.078125 to 0.078125
- down_bias: bfloat16 [2, 640], P(None, 'dp'), may hold values from -3 to 3
Outputs:
- final_stream: bfloat16 [16, 256, 640], P('dp')
- residues_grad: float32 [16, 256, 640], P('dp')
- attn_gain_grad: float32 [2, 640], P(None, 'dp')
- attn_shift_grad: float32 [2, 640], P(None, 'dp')
- qkv_weight_grad: float32 [2, 640, 1920], P(None, 'dp')
- query_bias_grad: float32 [2, 640], P(None, 'dp')
- value_bias_grad: float32 [2, 640], P(None, 'dp')
- out_weight_grad: float32 [2, 640, 640], P(None, 'dp')
- out_bias_grad: float32 [2, 640], P(None, 'dp')
- ffn_gain_grad: float32 [2, 640], P(None, 'dp')
- ffn_shift_grad: float32 [2, 640], P(None, 'dp')
- up_weight_grad: float32 [2, 640, 5120], P(None, 'dp')
- up_bias_grad: float32 [2, 5120], P(None, 'dp')
- down_weight_grad: float32 [2, 5120, 640], P(None, 'dp')
- down_bias_grad: float32 [2, 640], P(None, 'dp')
The draws below stay inside these ranges and needn't reach their ends.
Inputs may be any that keep to these rules, and one draw needn't show every extreme that they name: `key_lengths`: keys at positions at or beyond a crop's length are padding; some crop is 256 long. `masked`: marks only positions below the crop's length; each crop has its own marking rate.
All inputs are finite; a program needn't handle non-finite values.
Results may differ from the reference program's by a relative error of at most 0.018.
Values may be sent and summed in bfloat16 or wider, within the bound.
No kernel may reach another device: no remote copies, remote signals or barrier semaphores. Data moves between devices by JAX's collectives and lax.ppermute only.
A program may use at most 640 MiB of HBM per device.

```python
import math
import jax
import jax.numpy as jnp
from jax import lax

D = 640
HEADS = 20
HEAD_DIM = 32
FF = 5120
LAYERS = 2
LENGTH = 256
SEQS = 16


def shared_lengths(key):
    length_key = jax.random.fold_in(key, 101)
    drawn = jax.random.randint(length_key, (SEQS,), LENGTH // 2, LENGTH + 1)
    return drawn.at[0].set(LENGTH).astype(jnp.int32)


def draw_key_lengths(key, part):
    lengths = shared_lengths(key)
    return lengths


def draw_masked(key, part):
    lengths = shared_lengths(key)
    key = jax.random.fold_in(key, 2)
    rate_key, choose_key = jax.random.split(key)
    rates = jax.random.randint(rate_key, (SEQS, 1), 2, 9)
    picks = jax.random.randint(choose_key, (SEQS, LENGTH), 0, 32)
    places = jnp.arange(LENGTH, dtype=jnp.int32)[None, :]
    return ((picks < rates) & (places < lengths[:, None])).astype(jnp.int32)


def block_scale(own_key, dims, pieces, low, high):
    level, own = 1.0, jax.random.fold_in(own_key, 6)
    for dim, parts in pieces:
        draws = jnp.exp(jax.random.uniform(jax.random.fold_in(own, dim), (parts,), jnp.float32, low / len(pieces), high / len(pieces)))
        level = level * jnp.repeat(draws, dims[dim] // parts).reshape([-1 if axis == dim else 1 for axis in range(len(dims))])
    return level


def noise(rng, dims, scale, limit, shards=(), held_as=jnp.bfloat16):
    array = scale * jax.random.normal(rng, dims, jnp.float32)
    if shards:
        array = array * block_scale(rng, dims, shards, -0.22, 0.18)
    return jnp.clip(array, -limit, limit).astype(held_as)


def setup_inputs(seed: int = 0) -> dict:
    splits = jax.random.split(jax.random.key(seed), 18)
    residues = noise(splits[0], (SEQS, LENGTH, D), 1.0, 6.0, ((0, 8),))
    out_grad = noise(splits[1], (SEQS, LENGTH, D), 1.0, 6.0, ((0, 8),))
    key_lengths = draw_key_lengths(jax.random.fold_in(splits[17], 71), 0)
    masked = draw_masked(jax.random.fold_in(splits[17], 71), 0)
    attn_gain = jnp.clip(1.0 + 0.18 * jax.random.normal(splits[4], (LAYERS, D), jnp.float32), 0.099609375, 1.8984375).astype(jnp.bfloat16)
    attn_shift = noise(splits[5], (LAYERS, D), 0.5, 3.0, ((1, 8),))
    qkv_weight = noise(splits[6], (LAYERS, D, 3 * D), D ** -0.5, 0.25, ((1, 8),))
    query_bias = noise(splits[7], (LAYERS, D), 0.5, 3.0, ((1, 8),))
    value_bias = noise(splits[8], (LAYERS, D), 0.05, 0.29882812, ((1, 8),))
    out_weight = noise(splits[9], (LAYERS, D, D), (max(D // 128, 1)) ** -0.5, 2.5, ((1, 8),))
    out_bias = noise(splits[10], (LAYERS, D), 0.5, 3.0, ((1, 8),))
    ffn_gain = jnp.clip(1.0 + 0.18 * jax.random.normal(splits[11], (LAYERS, D), jnp.float32), 0.099609375, 1.8984375).astype(jnp.bfloat16)
    ffn_shift = noise(splits[12], (LAYERS, D), 0.5, 3.0, ((1, 8),))
    up_weight = noise(splits[13], (LAYERS, D, FF), D ** -0.5, 0.25, ((1, 8),))
    up_bias = noise(splits[14], (LAYERS, FF), 0.5, 3.0, ((1, 8),))
    down_weight = noise(splits[15], (LAYERS, FF, D), FF ** -0.5, 0.078125, ((1, 8),))
    down_bias = noise(splits[16], (LAYERS, D), 0.5, 3.0, ((1, 8),))
    return dict(residues=residues, out_grad=out_grad, key_lengths=key_lengths, masked=masked, attn_gain=attn_gain, attn_shift=attn_shift, qkv_weight=qkv_weight, query_bias=query_bias, value_bias=value_bias, out_weight=out_weight, out_bias=out_bias, ffn_gain=ffn_gain, ffn_shift=ffn_shift, up_weight=up_weight, up_bias=up_bias, down_weight=down_weight, down_bias=down_bias)


@jax.custom_vjp
def low(v):
    return lax.optimization_barrier(v.astype(jnp.bfloat16)).astype(jnp.float32)

@jax.custom_vjp
def low_back(v):
    return v

def low_keep(v):
    return (low(v), None)

def low_pass(kept, grad):
    return (grad,)

def back_keep(v):
    return (v, None)

def back_low(kept, grad):
    return (low(grad),)
low.defvjp(low_keep, low_pass)
low_back.defvjp(back_keep, back_low)
EPSILON = 1e-05
HIGHEST = lax.Precision.HIGHEST
ROOT_HALF = 0.7071067811865476
NEGATIVE = -1e+30

def layer_norm(stream, norm_gain, norm_shift):
    average = lax.optimization_barrier(jnp.mean(stream, axis=-1, keepdims=True))
    centered = stream - average
    variance = lax.optimization_barrier(jnp.mean(centered * centered, axis=-1, keepdims=True))
    return centered * lax.rsqrt(variance + EPSILON) * norm_gain + norm_shift

def gelu_exact(values):
    return 0.5 * values * (1.0 + lax.erf(values * ROOT_HALF))

def attention_block(stream, lengths, layer_weights):
    norm_gain, norm_shift, qkv_matrix, query_add, value_add, out_matrix, out_add = layer_weights
    group_size = stream.shape[0]
    normed = low(layer_norm(stream, norm_gain, norm_shift))
    projected = jnp.einsum('gld,de->gle', normed, qkv_matrix, precision=HIGHEST)
    projected = projected + jnp.concatenate([query_add, jnp.zeros_like(query_add), value_add])
    projected = low(low_back(projected))
    shaped = projected.reshape(group_size, LENGTH, 3, HEADS, HEAD_DIM)
    queries = shaped[:, :, 0]
    key_rows = shaped[:, :, 1]
    value_rows = shaped[:, :, 2]
    raw_scores = jnp.einsum('gqhc,gkhc->ghqk', queries, key_rows, precision=HIGHEST) * HEAD_DIM ** (-0.5)
    raw_scores = low_back(raw_scores)
    key_valid = jnp.arange(LENGTH, dtype=jnp.int32)[None, :] < lengths[:, None]
    scores = jnp.where(key_valid[:, None, None, :], raw_scores, NEGATIVE)
    largest = lax.optimization_barrier(jnp.max(scores, axis=-1, keepdims=True))
    exponent = jnp.exp(scores - largest)
    probabilities = low(exponent / lax.optimization_barrier(jnp.sum(exponent, axis=-1, keepdims=True)))
    context = jnp.einsum('ghqk,gkhc->gqhc', probabilities, value_rows, precision=HIGHEST)
    context = low(low_back(context.reshape(group_size, LENGTH, D)))
    branch = jnp.einsum('gld,de->gle', context, out_matrix, precision=HIGHEST) + out_add
    return stream + branch

def feed_forward_block(stream, layer_weights):
    norm_gain, norm_shift, up_matrix, up_add, down_matrix, down_add = layer_weights
    normed = low(layer_norm(stream, norm_gain, norm_shift))
    up_value = low_back(jnp.einsum('gld,df->glf', normed, up_matrix, precision=HIGHEST) + up_add)
    hidden = low(gelu_exact(up_value))
    return stream + jnp.einsum('glf,fd->gld', hidden, down_matrix, precision=HIGHEST) + down_add

def both_layers(stream, lengths, attn_params, ffn_params):
    for layer_index in range(LAYERS):
        stream = attention_block(stream, lengths, tuple((tensor[layer_index] for tensor in attn_params)))
        stream = low_back(low(stream))
        stream = feed_forward_block(stream, tuple((tensor[layer_index] for tensor in ffn_params)))
        if layer_index + 1 < LAYERS:
            stream = low_back(low(stream))
        else:
            stream = low(stream)
    return stream

def reference(residues, out_grad, key_lengths, masked, attn_gain, attn_shift, qkv_weight, query_bias, value_bias, out_weight, out_bias, ffn_gain, ffn_shift, up_weight, up_bias, down_weight, down_bias):
    attn_params = tuple((tensor.astype(jnp.float32) for tensor in (attn_gain, attn_shift, qkv_weight, query_bias, value_bias, out_weight, out_bias)))
    ffn_params = tuple((tensor.astype(jnp.float32) for tensor in (ffn_gain, ffn_shift, up_weight, up_bias, down_weight, down_bias)))
    group_size = math.gcd(SEQS, 8)
    group_count = SEQS // group_size
    stream = residues.astype(jnp.float32).reshape(group_count, group_size, LENGTH, D)
    lengths = key_lengths.astype(jnp.int32).reshape(group_count, group_size)
    checked = jax.checkpoint(both_layers)

    def whole(stream_all, attn_all, ffn_all):

        def scan_step(carried, inputs):
            return (carried, checked(inputs[0], inputs[1], attn_all, ffn_all))
        return lax.scan(scan_step, None, (stream_all, lengths))[1]
    final_rows, pullback = jax.vjp(whole, stream, attn_params, ffn_params)
    weighted = out_grad.astype(jnp.float32) * masked.astype(jnp.float32)[:, :, None]
    stream_grad, attn_grads, ffn_grads = pullback(weighted.reshape(group_count, group_size, LENGTH, D))
    return (final_rows.reshape(SEQS, LENGTH, D).astype(jnp.bfloat16), stream_grad.reshape(SEQS, LENGTH, D), attn_grads[0], attn_grads[1], attn_grads[2], attn_grads[3], attn_grads[4], attn_grads[5], attn_grads[6], ffn_grads[0], ffn_grads[1], ffn_grads[2], ffn_grads[3], ffn_grads[4], ffn_grads[5])
```

```python
import functools

import jax
import jax.numpy as jnp
from jax import lax
from jax.experimental import pallas as pl
from jax.experimental.pallas import tpu as pltpu
from jax.sharding import PartitionSpec as P

HEADS = 20
EPSILON = 1e-05
ROOT_HALF = 0.7071067811865476
INV_ROOT_TAU = 0.3989422804014327
NEGATIVE = -1e30
BF = jnp.bfloat16
F32 = jnp.float32
VMEM_LIMIT = 56 * 1024 * 1024


def dot_nn(a, b):
    return jnp.dot(a, b, preferred_element_type=F32)


def dot_nt(a, b):
    return lax.dot_general(a, b, (((1,), (1,)), ((), ())), preferred_element_type=F32)


def dot_tn(a, b):
    return lax.dot_general(a, b, (((0,), (0,)), ((), ())), preferred_element_type=F32)


def norm_parts(stream):
    average = jnp.mean(stream, axis=-1, keepdims=True)
    centered = stream - average
    reciprocal = lax.rsqrt(jnp.mean(centered * centered, axis=-1, keepdims=True) + EPSILON)
    return centered * reciprocal, reciprocal


def norm_back(grad_n, scaled, reciprocal, gain):
    inner = grad_n * gain
    return reciprocal * (
        inner
        - jnp.mean(inner, axis=-1, keepdims=True)
        - scaled * jnp.mean(inner * scaled, axis=-1, keepdims=True)
    )


def own_columns(ref, step, core, width):
    if step == 0:
        return ref[:, :width]
    return ref[:, pl.ds(pl.multiple_of(core * step, 128), step)][:, :width]


def column_sum(values):
    return jnp.sum(values, axis=0, keepdims=True)


def key_valid_column(ids_ref, half):
    length, core = ids_ref[0], ids_ref[1]
    place = lax.broadcasted_iota(jnp.int32, (2 * half, 1), 0)
    own = place + core * half
    sibling = place - half + (1 - core) * half
    return jnp.where(place < half, own, sibling) < length


def head_probs(queries, key_rows, valid):
    head_size = queries.shape[1]
    scores = dot_nt(key_rows, queries) * head_size ** (-0.5)
    scores = jnp.where(valid, scores, NEGATIVE)
    exponent = jnp.exp(scores - jnp.max(scores, axis=0, keepdims=True))
    return exponent * (1.0 / jnp.sum(exponent, axis=0, keepdims=True))


def key_valid_row(ids_ref, half):
    length, core = ids_ref[0], ids_ref[1]
    place = lax.broadcasted_iota(jnp.int32, (1, 2 * half), 1)
    own = place + core * half
    sibling = place - half + (1 - core) * half
    return jnp.where(place < half, own, sibling) < length


def attn_forward_kernel(
    heads, step, ids_ref, own_ref, sib_ref, gain_ref, shift_ref, w_ref, bias_ref, *refs
):
    proj_ref, ctx_ref = refs
    half = own_ref.shape[0]
    width = ctx_ref.shape[1]
    size = width // heads
    w = own_columns(w_ref, step, ids_ref[1], 3 * width)
    for row, ref in ((0, own_ref), (half, sib_ref)):
        scaled, _ = norm_parts(ref[...].astype(F32))
        normed = (scaled * gain_ref[...] + shift_ref[...]).astype(BF)
        proj_ref[row : row + half, :] = (dot_nn(normed, w) + bias_ref[...]).astype(BF)
    valid = key_valid_row(ids_ref, half)
    for h in range(heads):
        at = h * size
        queries = proj_ref[:, at : at + size]
        key_rows = proj_ref[:, width + at : width + at + size]
        scores = dot_nt(queries, key_rows) * size ** (-0.5)
        scores = jnp.where(valid, scores, NEGATIVE)
        exponent = jnp.exp(scores - jnp.max(scores, axis=-1, keepdims=True))
        probs = exponent * (1.0 / jnp.sum(exponent, axis=-1, keepdims=True))
        ctx_ref[:, at : at + size] = dot_nn(
            probs.astype(BF), proj_ref[:, 2 * width + at : 2 * width + at + size]
        ).astype(BF)


def out_kernel(
    out_at, ids_ref, ctx_ref, other_ref, own_ref, w_ref, bias_ref, gain_ref, shift_ref, *refs
):
    mid_ref, n2_ref = refs
    half = own_ref.shape[0]
    width = ctx_ref.shape[1]
    core = ids_ref[1]
    mine = pl.ds(pl.multiple_of(core * width, 64), width)
    theirs = pl.ds(pl.multiple_of((1 - core) * width, 64), width)
    columns = slice(out_at, out_at + own_ref.shape[1])
    total = dot_nn(ctx_ref[:half, :], w_ref[mine, columns])
    total = total + dot_nn(other_ref[half:, :], w_ref[theirs, columns])
    mid = (own_ref[...].astype(F32) + total + bias_ref[...]).astype(BF)
    mid_ref[...] = mid
    scaled, _ = norm_parts(mid.astype(F32))
    n2_ref[...] = (scaled * gain_ref[...] + shift_ref[...]).astype(BF)


def ff_tiles(width):
    tile = 256 if width % 256 == 0 else width
    return [(at, tile) for at in range(0, width, tile)]


def ffn_forward_kernel(count, *refs):
    x_refs = refs[:count]
    up_ref, upb_ref, down_ref = refs[count : count + 3]
    out_refs = refs[count + 3 : 2 * count + 3]
    acc_ref = refs[-1]
    rows = x_refs[0].shape[0]
    shift = up_ref.shape[1] - upb_ref.shape[1]
    x = jnp.concatenate([ref[...] for ref in x_refs], axis=0)
    for at, tile in ff_tiles(upb_ref.shape[1]):
        up = dot_nn(x, up_ref[:, shift + at : shift + at + tile]) + upb_ref[:, at : at + tile]
        hidden = (0.5 * up * (1.0 + lax.erf(up * ROOT_HALF))).astype(BF)
        part = dot_nn(hidden, down_ref[at : at + tile, :])
        if at == 0:
            acc_ref[...] = part
        else:
            acc_ref[...] += part
    for j, ref in enumerate(out_refs):
        ref[...] = acc_ref[j * rows : (j + 1) * rows, :].astype(BF)


def ffn_backward_kernel(count, *refs):
    x_refs, g_refs = refs[:count], refs[count : 2 * count]
    up_ref, upb_ref, down_ref = refs[2 * count : 2 * count + 3]
    q_refs = refs[2 * count + 3 : 3 * count + 3]
    hidden_ref, gup_ref, dupb_ref, qacc_ref = refs[3 * count + 3 :]
    rows = x_refs[0].shape[0]
    shift = up_ref.shape[1] - upb_ref.shape[1]
    x = jnp.concatenate([ref[...] for ref in x_refs], axis=0)
    g = jnp.concatenate([ref[...] for ref in g_refs], axis=0)
    for at, tile in ff_tiles(upb_ref.shape[1]):
        up_tile = up_ref[:, shift + at : shift + at + tile]
        up = dot_nn(x, up_tile) + upb_ref[:, at : at + tile]
        bell = 0.5 * (1.0 + lax.erf(up * ROOT_HALF))
        hidden_ref[:, at : at + tile] = (up * bell).astype(BF)
        slope = bell + up * INV_ROOT_TAU * jnp.exp(-0.5 * up * up)
        grad_up = (dot_nt(g, down_ref[at : at + tile, :]) * slope).astype(BF)
        gup_ref[:, at : at + tile] = grad_up
        dupb_ref[:, at : at + tile] = column_sum(grad_up.astype(F32))
        part = dot_nt(grad_up, up_tile)
        if at == 0:
            qacc_ref[...] = part
        else:
            qacc_ref[...] += part
    for j, ref in enumerate(q_refs):
        ref[...] = qacc_ref[j * rows : (j + 1) * rows, :].astype(BF)


def ffn_weights_kernel(count, *refs):
    ids_ref, refs = refs[0], refs[1:]
    x_refs, g_refs = refs[:count], refs[count : 2 * count]
    hidden_ref, gup_ref, down_ref = refs[2 * count : 2 * count + 3]
    rest = refs[2 * count + 3 :]
    own_ref, sib_ref, dup_ref = rest[:3]
    p_refs = rest[3:-1]
    ddown_ref = rest[-1]
    rows = x_refs[0].shape[0]
    width = gup_ref.shape[1]
    core, chip = ids_ref[1], ids_ref[2]
    x = jnp.concatenate([ref[...] for ref in x_refs], axis=0)
    g = jnp.concatenate([ref[...] for ref in g_refs], axis=0)
    turned = x.T
    for at, tile in ff_tiles(width):
        ddown_ref[at : at + tile, :] = dot_tn(hidden_ref[:, at : at + tile], g).astype(BF)
        dup_ref[:, at : at + tile] = dot_nn(turned, gup_ref[:, at : at + tile]).astype(BF)
    model = x.shape[1]
    part = width // 2
    piece = model // (2 * count)
    for side, ref in ((core, own_ref), (1 - core, sib_ref)):
        for j in range(count if piece % 16 == 0 else 0):
            at = pl.multiple_of((2 * (chip ^ j) + side) * piece, 16)
            ref[j * piece : (j + 1) * piece, :] = dup_ref[pl.ds(at, piece), :]
        base = side * part
        for b in range(width // model):
            at = pl.multiple_of(base + b * (model // 2), 16)
            ref[model // 2 :, b * model : (b + 1) * model] = ddown_ref[pl.ds(at, model // 2), :]
        for b in range(model // width):
            rows_at = slice(model // 2 + b * part, model // 2 + (b + 1) * part)
            columns = slice(b * width, (b + 1) * width)
            ref[rows_at, :] = ddown_ref[pl.ds(pl.multiple_of(base, 16), part), columns]
    for j, ref in enumerate(p_refs):
        hidden = hidden_ref[j * rows : (j + 1) * rows, :]
        ref[...] = dot_nn(hidden, down_ref[...]).astype(BF)


def ffn_norm_back_kernel(count, *refs):
    q_refs = refs[:count]
    mid_ref, g_ref, gain_ref, gm_ref, small_ref = refs[count:]
    grad_n = q_refs[0][...].astype(F32)
    for ref in q_refs[1:]:
        grad_n = grad_n + ref[...].astype(F32)
    scaled, reciprocal = norm_parts(mid_ref[...].astype(F32))
    g = g_ref[...].astype(F32)
    gm = (g + norm_back(grad_n, scaled, reciprocal, gain_ref[...])).astype(BF)
    gm_ref[...] = gm
    small_ref[0:1, :] = column_sum(gm.astype(F32))
    small_ref[1:2, :] = column_sum(grad_n * scaled)
    small_ref[2:3, :] = column_sum(grad_n)
    small_ref[3:4, :] = column_sum(g)


def attn_backward_kernel(
    heads,
    step,
    out_at,
    ids_ref,
    w_ref,
    proj_ref,
    gm_ref,
    gm_sib_ref,
    wout_ref,
    gproj_ref,
    gn_own_ref,
    gn_sib_ref,
    bias_ref,
    gctx_ref,
    turned_ref,
):
    half = gm_ref.shape[0]
    width = proj_ref.shape[1] // 3
    size = width // heads
    scale = size ** (-0.5)
    core = ids_ref[1]
    mine = pl.ds(pl.multiple_of(core * width, 64), width)
    w_out = wout_ref[mine, out_at : out_at + gm_ref.shape[1]]
    for row, ref in ((0, gm_ref), (half, gm_sib_ref)):
        gctx_ref[row : row + half, :] = dot_nt(ref[...], w_out).astype(BF)
    valid = key_valid_column(ids_ref, half)
    for h in range(heads):
        at = h * size
        q_at, k_at, v_at = (slice(s * width + at, s * width + at + size) for s in range(3))
        queries, key_rows, value_rows = proj_ref[:, q_at], proj_ref[:, k_at], proj_ref[:, v_at]
        probs = head_probs(queries, key_rows, valid)
        gctx = gctx_ref[:, at : at + size]
        grad_probs = dot_nt(value_rows, gctx)
        inner = jnp.sum(probs * grad_probs, axis=0, keepdims=True)
        grad_scores = (probs * (grad_probs - inner)).astype(BF)
        turned_ref[at : at + size, :] = dot_tn(key_rows, grad_scores) * scale
        gproj_ref[:, k_at] = (dot_nn(grad_scores, queries) * scale).astype(BF)
        gproj_ref[:, v_at] = dot_nn(probs.astype(BF), gctx).astype(BF)
    gproj_ref[:, :width] = turned_ref[...].T.astype(BF)
    bias_ref[...] = column_sum(gproj_ref[...].astype(F32))
    grad_n = dot_nt(gproj_ref[...], own_columns(w_ref, step, core, 3 * width))
    gn_own_ref[...] = grad_n[:half, :]
    gn_sib_ref[...] = grad_n[half:, :].astype(BF)


def attn_weights_kernel(
    count,
    ids_ref,
    own_ref,
    sib_ref,
    gain_ref,
    shift_ref,
    ctx_ref,
    other_ref,
    gm_ref,
    gm_sib_ref,
    gproj_ref,
    *refs,
):
    out_refs, full_ref = refs[:-1], refs[-1]
    half = own_ref.shape[0]
    width = ctx_ref.shape[1]
    core, chip = ids_ref[1], ids_ref[2]
    gm = jnp.concatenate([gm_ref[...], gm_sib_ref[...]], axis=0)
    middle = gm.shape[1] // 2
    gm_part = jnp.where(core == 0, gm[:, :middle].astype(F32), gm[:, middle:].astype(F32)).astype(BF)
    other = jnp.concatenate([other_ref[half:, :], other_ref[:half, :]], axis=0)
    mine = pl.ds(pl.multiple_of(core * width, 64), width)
    theirs = pl.ds(pl.multiple_of((1 - core) * width, 64), width)
    full_ref[mine, 3 * width :] = dot_tn(ctx_ref[...], gm_part).astype(BF)
    full_ref[theirs, 3 * width :] = dot_tn(other, gm_part).astype(BF)
    stream = jnp.concatenate([own_ref[...], sib_ref[...]], axis=0)
    scaled, _ = norm_parts(stream.astype(F32))
    normed = (scaled * gain_ref[...] + shift_ref[...]).astype(BF)
    full_ref[:, : 3 * width] = dot_tn(normed, gproj_ref[...]).astype(BF)
    if len(out_refs) == count:
        rows = out_refs[0].shape[0]
        for j, ref in enumerate(out_refs):
            ref[...] = full_ref[pl.ds(pl.multiple_of((chip ^ j) * rows, 16), rows), :]
    else:
        out_refs[0][...] = full_ref[...]


def attn_norm_back_kernel(gn_ref, recv_ref, own_ref, gm_ref, gain_ref, gs_ref, small_ref):
    grad_n = gn_ref[...] + recv_ref[...].astype(F32)
    scaled, reciprocal = norm_parts(own_ref[...].astype(F32))
    term = norm_back(grad_n, scaled, reciprocal, gain_ref[...])
    gs_ref[...] = (gm_ref[...].astype(F32) + term).astype(BF)
    small_ref[0:1, :] = column_sum(grad_n * scaled)
    small_ref[1:2, :] = column_sum(grad_n)


def pack_kernel(step, count, places_ref, qkv_ref, out_ref, up_ref, *refs):
    small_refs, (mine_ref, theirs_ref, rest_ref) = refs[:8], refs[8:11]
    chip, share = places_ref[1], up_ref.shape[2] // count
    for j, ref in enumerate(refs[11:]):
        ref[:, : out_ref.shape[2]] = out_ref[0]
        at = pl.multiple_of((chip ^ j) * share, 128)
        ref[:, out_ref.shape[2] :] = up_ref[0, :, pl.ds(at, share)]
    width = out_ref.shape[2]
    cols = width // 2
    core = places_ref[0]

    def columns(l, c):
        return jnp.concatenate(
            [qkv_ref[l, :, s * width + c * cols : s * width + (c + 1) * cols] for s in range(3)],
            axis=1,
        )

    first, second = columns(0, 0).astype(F32), columns(0, 1).astype(F32)
    smalls = jnp.concatenate([ref[...].astype(F32) for ref in small_refs], axis=0).T.astype(BF)
    for flag, ref in ((core == 0, mine_ref), (core != 0, theirs_ref)):
        ref[:, : 3 * cols] = jnp.where(flag, first, second).astype(BF)
        ref[:, 3 * cols :] = smalls
    rest_ref[...] = jnp.zeros_like(rest_ref)
    for c in range(2):
        rest_ref[:, c * step : c * step + 3 * cols] = columns(1, c)
    rest_ref[:, 2 * step :] = out_ref[1]


def run(micros, kernel, outs, operands, scratch=(), smem=0):
    vmem = pl.BlockSpec(memory_space=pltpu.VMEM)
    specs = [pl.BlockSpec(memory_space=pltpu.SMEM)] * smem + [vmem] * (len(operands) - smem)
    moved = sum(o.size * o.dtype.itemsize for o in list(operands) + list(outs))
    return pl.pallas_call(
        kernel,
        out_shape=[jax.ShapeDtypeStruct(o.shape, o.dtype) for o in outs],
        in_specs=specs,
        out_specs=[vmem] * len(outs),
        scratch_shapes=[pltpu.VMEM(shape, dtype) for shape, dtype in scratch],
        cost_estimate=pl.CostEstimate(
            flops=int(micros * 1.1e9), bytes_accessed=moved, transcendentals=0
        ),
        compiler_params=pltpu.CompilerParams(vmem_limit_bytes=VMEM_LIMIT),
    )(*operands)


def like(shape, dtype):
    return jax.ShapeDtypeStruct(shape, dtype)


def swap(x, axis, bit):
    size = lax.axis_size(axis)
    return lax.ppermute(x, axis, [(i, i ^ bit) for i in range(size)])


def to_sibling(x):
    return swap(x, "dp", 1)


def swap_chip(x, j):
    return swap(x, "dp", 2 * j)


def pick(x, index):
    return lax.dynamic_index_in_dim(x, index, 0, keepdims=False)


def in_order(parts, index):
    parts, bit = list(parts), 1
    while bit < len(parts):
        flag = (index & bit) != 0
        parts = [jnp.where(flag, parts[i ^ bit], parts[i]) for i in range(len(parts))]
        bit *= 2
    return parts


def spread(x, count):
    return [x] + [swap_chip(x, j) for j in range(1, count)]


def trade(blocks, chip, count):
    return [pick(blocks, chip)] + [swap_chip(pick(blocks, chip ^ j), j) for j in range(1, count)]


def total(parts):
    return functools.reduce(lambda a, b: a + b, [p.astype(F32) for p in parts])


def section_sum(x, z):
    low, high = z % 2, z // 2
    x = x.reshape((2, 2, x.shape[0] // 4) + x.shape[1:])
    half = total([pick(x, low), swap(pick(x, 1 - low), "section", 1)]).astype(BF)
    quarter = total([pick(half, high), swap(pick(half, 1 - high), "section", 2)]).astype(BF)
    half = jnp.stack(in_order([quarter, swap(quarter, "section", 2)], high))
    whole = jnp.stack(in_order([half, swap(half, "section", 1)], low))
    return whole.reshape((-1,) + x.shape[3:])


def section_streams(own, z, core):
    far = swap(own, "section", 2)
    near = swap(jnp.stack([own, far]), "section", 1)
    crops = in_order([own, near[0], far, near[1]], z)
    mine = jnp.where(core == 0, jnp.stack(crops[:2]), jnp.stack(crops[2:]))
    theirs = jnp.where(core == 0, jnp.stack(crops[2:]), jnp.stack(crops[:2]))
    recv = to_sibling(theirs)
    return jnp.concatenate(
        [jnp.where(core == 0, mine, recv), jnp.where(core == 0, recv, mine)], axis=1
    )


def after(x, *others):
    return lax.optimization_barrier((x, *others))[0]


def shards(
    residues,
    out_grad,
    key_lengths,
    masked,
    attn_gain,
    attn_shift,
    qkv_weight,
    query_bias,
    value_bias,
    out_weight,
    out_bias,
    ffn_gain,
    ffn_shift,
    up_weight,
    up_bias,
    down_weight,
    down_bias,
):
    data_count = lax.axis_size("dp")
    count = data_count // 2
    z = lax.axis_index("section")
    device = lax.axis_index("dp")
    core, chip = device % 2, device // 2
    layers, piece, triple = qkv_weight.shape
    width = triple // 3
    ff = up_weight.shape[2]
    ff_chip = ff // count
    heads = HEADS // 2
    cols = width // 2
    length = residues.shape[1]
    half = length // 2
    holder = core == z // 2
    vectors = 8
    step = -(-3 * cols // 128) * 128
    row = like((half, width), BF)

    smalls = [
        attn_gain,
        attn_shift,
        query_bias,
        value_bias,
        out_bias,
        ffn_gain,
        ffn_shift,
        down_bias,
    ]
    places = jnp.stack([core, chip]).astype(jnp.int32)
    packed = like((piece, 3 * cols + layers * vectors), BF)
    aligned = ff_chip % 128 == 0
    qkv_mine, qkv_theirs, rest1, *feed0 = run(
        2.2,
        functools.partial(pack_kernel, step, count),
        [packed, packed, like((piece, 2 * step + width), BF)]
        + [like((piece, width + ff_chip), BF)] * (count if aligned else 0),
        [places, qkv_weight, out_weight, up_weight, *smalls],
        smem=1,
    )
    if not aligned:
        feed0 = [
            jnp.concatenate(
                [out_weight[0], lax.dynamic_slice_in_dim(up_weight[0], (chip ^ j) * ff_chip, ff_chip, 1)],
                axis=1,
            )
            for j in range(count)
        ]
    pair = jnp.stack(in_order([qkv_mine, to_sibling(qkv_theirs)], core))

    residues, out_grad, key_lengths = lax.optimization_barrier(
        (residues, out_grad, key_lengths, qkv_theirs)
    )[:3]
    length_own = lax.dynamic_slice_in_dim(key_lengths, z % 2, 1, 0)
    length_here = jnp.where(holder, length_own, to_sibling(length_own))
    ids = jnp.concatenate([length_here, places])
    stream0 = pick(residues, z % 2)
    grad0 = pick(out_grad, z % 2) * pick(masked, z % 2).astype(BF)[:, None]
    stream_recv = to_sibling(stream0)
    grad_recv = to_sibling(lax.dynamic_slice_in_dim(grad0, (1 - core) * half, half, 0))
    stream0 = jnp.where(holder, stream0, stream_recv)
    g_top = jnp.where(holder, lax.dynamic_slice_in_dim(grad0, core * half, half, 0), grad_recv)
    own = lax.dynamic_slice_in_dim(stream0, core * half, half, 0)
    sib = lax.dynamic_slice_in_dim(stream0, (1 - core) * half, half, 0)

    qkv0 = jnp.stack(in_order(spread(pair, count), chip))
    qkv0 = qkv0.reshape(width, 3 * cols + layers * vectors)
    small_full = qkv0[:, 3 * cols :].T.astype(F32)
    small_full = jnp.swapaxes(small_full.reshape(vectors, layers, 1, width), 0, 1)

    def trade_up(l, dep):
        own_up = after(up_weight[l], dep)

        def block(i):
            return lax.dynamic_slice_in_dim(own_up, i * ff_chip, ff_chip, 1)

        return [block(chip)] + [swap_chip(block(chip ^ j), j) for j in range(1, count)]

    def join(parts):
        got = jnp.stack(in_order(parts, chip))
        both = jnp.stack(in_order([got, to_sibling(got)], core), axis=1)
        return both.reshape(width, -1)

    def chip_rows(own_down):
        return jnp.concatenate(in_order([own_down, to_sibling(own_down)], core), axis=0)

    feed0 = [feed0[0]] + [swap_chip(feed0[j], j) for j in range(1, count)]
    own, *feed0 = lax.optimization_barrier((own, *feed0))
    g_sent = spread(after(g_top, qkv0), count)
    upb = jnp.concatenate(in_order([up_bias, to_sibling(up_bias)], core), axis=1).astype(F32)
    zero_cols = jnp.zeros((1, cols), F32)

    def vec(l, i):
        return small_full[l, i]

    def core_bias(l):
        q = jnp.where(core == 0, vec(l, 2)[:, :cols], vec(l, 2)[:, cols:])
        v = jnp.where(core == 0, vec(l, 3)[:, :cols], vec(l, 3)[:, cols:])
        return jnp.concatenate([q, zero_cols, v], axis=1)

    qkv_full, qkv_step, out_at = [qkv0, None], [0, step], [0, 2 * step]
    up_full, down_full, out_full = [None, None], [None, None], [None, None]
    saved = []
    for l in range(layers):
        proj, ctx = run(
            6,
            functools.partial(attn_forward_kernel, heads, qkv_step[l]),
            [like((length, 3 * cols), BF), like((length, cols), BF)],
            [ids, own, sib, vec(l, 0), vec(l, 1), qkv_full[l], core_bias(l)],
            smem=1,
        )
        if l == 0:
            ctx, *g_parts = lax.optimization_barrier((ctx, *g_sent))
            out_full[0] = up_full[0] = join(feed0)
            down_full[0] = chip_rows(after(down_weight[0], own))
            rest1 = lax.all_gather(after(rest1, ctx), "dp", axis=0, tiled=True)
            qkv_full[1] = out_full[1] = rest1
        else:
            ctx, *up1 = lax.optimization_barrier((ctx, *up1))
            up_full[1] = join(up1)
            down_full[1] = chip_rows(after(down_weight[1], own))
        other = to_sibling(ctx)
        mid, normed2 = run(
            2.6,
            functools.partial(out_kernel, out_at[l]),
            [row, row],
            [ids, ctx, other, own, out_full[l], vec(l, 4), vec(l, 5), vec(l, 6)],
            smem=1,
        )
        parts = spread(normed2, count)
        saved.append((own, sib, proj, ctx, other, mid, parts))
        if l + 1 < layers:
            sums = run(
                6,
                functools.partial(ffn_forward_kernel, count),
                [row] * count,
                [*parts, up_full[l], upb[l][None], down_full[l]],
                scratch=[((count * half, width), F32)],
            )
            got = [sums[0]] + [swap_chip(sums[j], j) for j in range(1, count)]
            own = (total([mid, *got]) + vec(l, 7)).astype(BF)
            sib = to_sibling(own)
            up1 = trade_up(1, own)

    small_grads, upb_grads, ffn_grads, attn_grads = {}, {}, {}, {}
    for l in reversed(range(layers)):
        own, sib, proj, ctx, other, mid, parts = saved[l]
        top = l + 1 == layers
        wide = like((count * half, ff_chip), BF)
        results = run(
            8.3,
            functools.partial(ffn_backward_kernel, count),
            [row] * count + [wide, wide, like((1, ff_chip), F32)],
            [*parts, *g_parts, up_full[l], upb[l][None], down_full[l]],
            scratch=[((count * half, width), F32)],
        )
        sums, (hidden, grad_up, upb_grads[l]) = results[:count], results[count:]
        got = [sums[0]] + [swap_chip(sums[j], j) for j in range(1, count)]
        form = like((width, ff_chip), BF)
        fw_own, fw_sib, dup, *outs = run(
            5,
            functools.partial(ffn_weights_kernel, count),
            [form, form, form] + ([row] * count if top else []),
            [ids, *parts, *g_parts, hidden, grad_up, down_full[l]],
            scratch=[((ff_chip, width), BF)],
            smem=1,
        )
        if piece % 16 != 0:
            by_core = jnp.moveaxis(dup.reshape(count, 2, piece, ff_chip), 1, 0)
            order = jnp.arange(count) ^ chip
            blocks = [
                jnp.take(pick(by_core, c), order, axis=0).reshape(cols, ff_chip)
                for c in (core, 1 - core)
            ]
            fw_own = jnp.concatenate([blocks[0], fw_own[cols:]], axis=0)
            fw_sib = jnp.concatenate([blocks[1], fw_sib[cols:]], axis=0)
        got[1] = after(got[1], fw_own)
        if not top:
            final_got = lax.optimization_barrier((*final_got, sums[0]))[:-1]
            final = (total([final_mid, *final_got]) + vec(1, 7)).astype(BF)
            final_stream = section_streams(final, z, core)
        grad_mid, small_ffn = run(
            2.3,
            functools.partial(ffn_norm_back_kernel, count),
            [row, like((4, width), F32)],
            [*got, mid, g_parts[0], vec(l, 5)],
        )
        gm_sib = to_sibling(grad_mid)
        fw_recv = to_sibling(after(fw_sib, grad_mid))
        if top:
            outs = lax.optimization_barrier((*outs, gm_sib))[:-1]
            final_got = [outs[0]] + [swap_chip(outs[j], j) for j in range(1, count)]
            final_mid = mid

        gproj, gn_own, gn_sib, gproj_sum = run(
            8,
            functools.partial(attn_backward_kernel, heads, qkv_step[l], out_at[l]),
            [like((length, 3 * cols), BF), like((half, width), F32), row, like((1, 3 * cols), F32)],
            [ids, qkv_full[l], proj, grad_mid, gm_sib, out_full[l]],
            scratch=[((length, cols), BF), ((cols, length), F32)],
            smem=1,
        )
        gn_recv = to_sibling(gn_sib)
        fw_sum = total([fw_own, fw_recv]).astype(BF)
        gn_recv, fw_sum = lax.optimization_barrier((gn_recv, fw_sum))
        if top:
            ffn_grads[1] = lax.psum(fw_sum, "section")
        else:
            order = [list(reversed(range(lax.axis_size("section"))))]
            up_sum = lax.psum(fw_sum[:cols], "section", axis_index_groups=order)
        block_form = 2 * piece % 16 == 0
        packed = run(
            3.8,
            functools.partial(attn_weights_kernel, count),
            [like((2 * piece, 4 * cols), BF)] * count
            if block_form
            else [like((width, 4 * cols), BF)],
            [ids, own, sib, vec(l, 0), vec(l, 1), ctx, other, grad_mid, gm_sib, gproj],
            scratch=[((width, 4 * cols), BF)],
            smem=1,
        )
        if not block_form:
            packed = packed[0].reshape(count, 2 * piece, 4 * cols)
            packed = [pick(packed, chip ^ j) for j in range(count)]
        grad_stream, small_attn = run(
            2.2,
            attn_norm_back_kernel,
            [row, like((2, width), F32)],
            [gn_own, gn_recv, own, grad_mid, vec(l, 0)],
        )
        if top:
            g_parts = spread(grad_stream, count)
            packed = list(lax.optimization_barrier((*packed, *g_parts)))
            packed, g_parts = packed[:count], packed[count:]
        else:
            residues_grad = section_streams(grad_stream, z, core).astype(F32)
        sent = [packed[0]] + [swap_chip(packed[j], j) for j in range(1, count)]

        def chip_sum(sent):
            packed = total(sent).astype(BF).reshape(2, piece, 4 * cols)
            mine, theirs = pick(packed, core), pick(packed, 1 - core)
            both = jnp.stack(in_order([mine, to_sibling(theirs)], core))
            return both.reshape(2 * piece, 4 * cols)

        if top:
            sent_top, sum_top = sent, chip_sum
        else:
            down_sum = section_sum(fw_sum[cols:], z)
            sent_top = lax.optimization_barrier((*sent_top, grad_stream))[:-1]
            sent = list(lax.optimization_barrier((*sent, grad_stream))[:-1])
            attn_grads[1] = section_sum(sum_top(sent_top), z)
            both, up_sum, ffn_grads[1] = lax.optimization_barrier(
                (chip_sum(sent), up_sum, ffn_grads[1])
            )
            attn_grads[0] = lax.psum(both, "section")
            start = after(ffn_grads[1], grad_stream)
            ffn_blocks = {
                1: (start[:cols], start[cols:]),
                0: (up_sum, down_sum),
            }
        q_sum, v_sum = gproj_sum[:, :cols], gproj_sum[:, 2 * cols :]
        spread_out = [
            jnp.where(core == 0, jnp.concatenate([s, zero_cols], 1), jnp.concatenate([zero_cols, s], 1))
            for s in (q_sum, v_sum)
        ]
        small_grads[l] = jnp.concatenate([small_attn, *spread_out, small_ffn], axis=0)

    packed = jnp.stack([small_grads[l] for l in range(layers)])
    packed = jnp.transpose(
        packed.reshape(layers, vectors, count, 2, piece), (2, 3, 0, 1, 4)
    ).reshape(count, 2, layers * vectors * piece)
    packed = total(trade(packed, chip, count))
    biases = jnp.stack([upb_grads[l] for l in range(layers)]).reshape(layers, 2, ff_chip // 2)
    biases = jnp.transpose(biases, (1, 0, 2)).reshape(2, layers * (ff_chip // 2))
    packed = jnp.concatenate([packed, biases], axis=1)
    packed = pick(packed, core) + to_sibling(pick(packed, 1 - core))
    one = packed + swap(packed, "section", 1)
    packed = one + swap(one, "section", 2)
    split = layers * vectors * piece
    grads = packed[:split].reshape(layers, vectors, piece)
    up_bias_grad = packed[split:].reshape(layers, ff_chip // 2)

    def weights(l):
        both = attn_grads[l].reshape(2, piece, 4, cols)
        qkv = jnp.transpose(both[:, :, :3], (1, 2, 0, 3)).reshape(piece, triple)
        out = jnp.transpose(both[:, :, 3], (1, 0, 2)).reshape(piece, width)
        blocks, down = ffn_blocks[l]
        blocks = [blocks[j * piece : (j + 1) * piece] for j in range(count)]
        up = in_order([blocks[0]] + [swap_chip(blocks[j], j) for j in range(1, count)], chip)
        if ff_chip >= width:
            down = [down[:, b : b + width] for b in range(0, ff_chip, width)]
            down = jnp.concatenate(down, axis=0)
        else:
            rows = ff_chip // 2
            down = [down[b : b + rows] for b in range(0, cols, rows)]
            down = jnp.concatenate(down, axis=1)
        return qkv, out, jnp.concatenate(up, axis=1), down

    per_layer = [weights(l) for l in range(layers)]
    stacked = [jnp.stack([p[i] for p in per_layer]).astype(F32) for i in range(4)]
    return (
        final_stream,
        residues_grad,
        grads[:, 0],
        grads[:, 1],
        stacked[0],
        grads[:, 2],
        grads[:, 3],
        stacked[1],
        grads[:, 4],
        grads[:, 5],
        grads[:, 6],
        stacked[2],
        up_bias_grad,
        stacked[3],
        grads[:, 7],
    )


def solution(mesh):
    rows, vector, matrix = P("dp", None, None), P(None, "dp"), P(None, "dp", None)
    weights = (
        vector,
        vector,
        matrix,
        vector,
        vector,
        matrix,
        vector,
        vector,
        vector,
        matrix,
        vector,
        matrix,
        vector,
    )
    return jax.shard_map(
        shards,
        mesh=mesh,
        in_specs=(rows, rows, P("dp"), P("dp", None), *weights),
        out_specs=(rows, rows, *weights),
        check_vma=False,
    )
```

```python
import functools

import jax
import jax.numpy as jnp
from jax import lax
from jax.experimental import pallas as pl
from jax.experimental.pallas import tpu as pltpu
from jax.sharding import PartitionSpec as P

HEADS = 20
EPSILON = 1e-05
ROOT_HALF = 0.7071067811865476
INV_ROOT_TAU = 0.3989422804014327
NEGATIVE = -1e30
BF = jnp.bfloat16
F32 = jnp.float32
VMEM_LIMIT = 56 * 1024 * 1024


def dot_nn(a, b):
    return jnp.dot(a, b, preferred_element_type=F32)


def dot_nt(a, b):
    return lax.dot_general(a, b, (((1,), (1,)), ((), ())), preferred_element_type=F32)


def dot_tn(a, b):
    return lax.dot_general(a, b, (((0,), (0,)), ((), ())), preferred_element_type=F32)


def norm_parts(stream):
    average = jnp.mean(stream, axis=-1, keepdims=True)
    centered = stream - average
    reciprocal = lax.rsqrt(jnp.mean(centered * centered, axis=-1, keepdims=True) + EPSILON)
    return centered * reciprocal, reciprocal


def norm_back(grad_n, scaled, reciprocal, gain):
    inner = grad_n * gain
    return reciprocal * (
        inner
        - jnp.mean(inner, axis=-1, keepdims=True)
        - scaled * jnp.mean(inner * scaled, axis=-1, keepdims=True)
    )


def own_columns(ref, step, core, width):
    if step == 0:
        return ref[:, :width]
    return ref[:, pl.ds(pl.multiple_of(core * step, 128), step)][:, :width]


def column_sum(values):
    return jnp.sum(values, axis=0, keepdims=True)


def key_valid_column(ids_ref, half):
    length, core = ids_ref[0], ids_ref[1]
    place = lax.broadcasted_iota(jnp.int32, (2 * half, 1), 0)
    own = place + core * half
    sibling = place - half + (1 - core) * half
    return jnp.where(place < half, own, sibling) < length


def head_probs(queries, key_rows, valid):
    head_size = queries.shape[1]
    scores = dot_nt(key_rows, queries) * head_size ** (-0.5)
    scores = jnp.where(valid, scores, NEGATIVE)
    exponent = jnp.exp(scores - jnp.max(scores, axis=0, keepdims=True))
    return exponent * (1.0 / jnp.sum(exponent, axis=0, keepdims=True))


def key_valid_row(ids_ref, half):
    length, core = ids_ref[0], ids_ref[1]
    place = lax.broadcasted_iota(jnp.int32, (1, 2 * half), 1)
    own = place + core * half
    sibling = place - half + (1 - core) * half
    return jnp.where(place < half, own, sibling) < length


def attn_forward_kernel(
    heads, step, ids_ref, own_ref, sib_ref, gain_ref, shift_ref, w_ref, bias_ref, *refs
):
    proj_ref, ctx_ref = refs
    half = own_ref.shape[0]
    width = ctx_ref.shape[1]
    size = width // heads
    w = own_columns(w_ref, step, ids_ref[1], 3 * width)
    for row, ref in ((0, own_ref), (half, sib_ref)):
        scaled, _ = norm_parts(ref[...].astype(F32))
        normed = (scaled * gain_ref[...] + shift_ref[...]).astype(BF)
        proj_ref[row : row + half, :] = (dot_nn(normed, w) + bias_ref[...]).astype(BF)
    valid = key_valid_row(ids_ref, half)
    for h in range(heads):
        at = h * size
        queries = proj_ref[:, at : at + size]
        key_rows = proj_ref[:, width + at : width + at + size]
        scores = dot_nt(queries, key_rows) * size ** (-0.5)
        scores = jnp.where(valid, scores, NEGATIVE)
        exponent = jnp.exp(scores - jnp.max(scores, axis=-1, keepdims=True))
        probs = exponent * (1.0 / jnp.sum(exponent, axis=-1, keepdims=True))
        ctx_ref[:, at : at + size] = dot_nn(
            probs.astype(BF), proj_ref[:, 2 * width + at : 2 * width + at + size]
        ).astype(BF)


def out_kernel(
    out_at, ids_ref, ctx_ref, other_ref, own_ref, w_ref, bias_ref, gain_ref, shift_ref, *refs
):
    mid_ref, n2_ref = refs
    half = own_ref.shape[0]
    width = ctx_ref.shape[1]
    core = ids_ref[1]
    mine = pl.ds(pl.multiple_of(core * width, 64), width)
    theirs = pl.ds(pl.multiple_of((1 - core) * width, 64), width)
    columns = slice(out_at, out_at + own_ref.shape[1])
    total = dot_nn(ctx_ref[:half, :], w_ref[mine, columns])
    total = total + dot_nn(other_ref[half:, :], w_ref[theirs, columns])
    mid = (own_ref[...].astype(F32) + total + bias_ref[...]).astype(BF)
    mid_ref[...] = mid
    scaled, _ = norm_parts(mid.astype(F32))
    n2_ref[...] = (scaled * gain_ref[...] + shift_ref[...]).astype(BF)


def ff_tiles(width):
    tile = 256 if width % 256 == 0 else width
    return [(at, tile) for at in range(0, width, tile)]


def ffn_forward_kernel(count, *refs):
    x_refs = refs[:count]
    up_ref, upb_ref, down_ref = refs[count : count + 3]
    out_refs = refs[count + 3 : 2 * count + 3]
    acc_ref = refs[-1]
    rows = x_refs[0].shape[0]
    shift = up_ref.shape[1] - upb_ref.shape[1]
    x = jnp.concatenate([ref[...] for ref in x_refs], axis=0)
    for at, tile in ff_tiles(upb_ref.shape[1]):
        up = dot_nn(x, up_ref[:, shift + at : shift + at + tile]) + upb_ref[:, at : at + tile]
        hidden = (0.5 * up * (1.0 + lax.erf(up * ROOT_HALF))).astype(BF)
        part = dot_nn(hidden, down_ref[at : at + tile, :])
        if at == 0:
            acc_ref[...] = part
        else:
            acc_ref[...] += part
    for j, ref in enumerate(out_refs):
        ref[...] = acc_ref[j * rows : (j + 1) * rows, :].astype(BF)


def ffn_backward_kernel(count, *refs):
    x_refs, g_refs = refs[:count], refs[count : 2 * count]
    up_ref, upb_ref, down_ref = refs[2 * count : 2 * count + 3]
    q_refs = refs[2 * count + 3 : 3 * count + 3]
    hidden_ref, gup_ref, dupb_ref, qacc_ref = refs[3 * count + 3 :]
    rows = x_refs[0].shape[0]
    shift = up_ref.shape[1] - upb_ref.shape[1]
    x = jnp.concatenate([ref[...] for ref in x_refs], axis=0)
    g = jnp.concatenate([ref[...] for ref in g_refs], axis=0)
    for at, tile in ff_tiles(upb_ref.shape[1]):
        up_tile = up_ref[:, shift + at : shift + at + tile]
        up = dot_nn(x, up_tile) + upb_ref[:, at : at + tile]
        bell = 0.5 * (1.0 + lax.erf(up * ROOT_HALF))
        hidden_ref[:, at : at + tile] = (up * bell).astype(BF)
        slope = bell + up * INV_ROOT_TAU * jnp.exp(-0.5 * up * up)
        grad_up = (dot_nt(g, down_ref[at : at + tile, :]) * slope).astype(BF)
        gup_ref[:, at : at + tile] = grad_up
        dupb_ref[:, at : at + tile] = column_sum(grad_up.astype(F32))
        part = dot_nt(grad_up, up_tile)
        if at == 0:
            qacc_ref[...] = part
        else:
            qacc_ref[...] += part
    for j, ref in enumerate(q_refs):
        ref[...] = qacc_ref[j * rows : (j + 1) * rows, :].astype(BF)


def ffn_weights_kernel(count, *refs):
    ids_ref, refs = refs[0], refs[1:]
    x_refs, g_refs = refs[:count], refs[count : 2 * count]
    hidden_ref, gup_ref, down_ref = refs[2 * count : 2 * count + 3]
    rest = refs[2 * count + 3 :]
    own_ref, sib_ref, dup_ref = rest[:3]
    p_refs = rest[3:-1]
    ddown_ref = rest[-1]
    rows = x_refs[0].shape[0]
    width = gup_ref.shape[1]
    core, chip = ids_ref[1], ids_ref[2]
    x = jnp.concatenate([ref[...] for ref in x_refs], axis=0)
    g = jnp.concatenate([ref[...] for ref in g_refs], axis=0)
    turned = x.T
    for at, tile in ff_tiles(width):
        ddown_ref[at : at + tile, :] = dot_tn(hidden_ref[:, at : at + tile], g).astype(BF)
        dup_ref[:, at : at + tile] = dot_nn(turned, gup_ref[:, at : at + tile]).astype(BF)
    model = x.shape[1]
    part = width // 2
    piece = model // (2 * count)
    for side, ref in ((core, own_ref), (1 - core, sib_ref)):
        for j in range(count if piece % 16 == 0 else 0):
            at = pl.multiple_of((2 * (chip ^ j) + side) * piece, 16)
            ref[j * piece : (j + 1) * piece, :] = dup_ref[pl.ds(at, piece), :]
        base = side * part
        for b in range(width // model):
            at = pl.multiple_of(base + b * (model // 2), 16)
            ref[model // 2 :, b * model : (b + 1) * model] = ddown_ref[pl.ds(at, model // 2), :]
        for b in range(model // width):
            rows_at = slice(model // 2 + b * part, model // 2 + (b + 1) * part)
            columns = slice(b * width, (b + 1) * width)
            ref[rows_at, :] = ddown_ref[pl.ds(pl.multiple_of(base, 16), part), columns]
    for j, ref in enumerate(p_refs):
        hidden = hidden_ref[j * rows : (j + 1) * rows, :]
        ref[...] = dot_nn(hidden, down_ref[...]).astype(BF)


def ffn_norm_back_kernel(count, *refs):
    q_refs = refs[:count]
    mid_ref, g_ref, gain_ref, gm_ref, small_ref = refs[count:]
    grad_n = q_refs[0][...].astype(F32)
    for ref in q_refs[1:]:
        grad_n = grad_n + ref[...].astype(F32)
    scaled, reciprocal = norm_parts(mid_ref[...].astype(F32))
    g = g_ref[...].astype(F32)
    gm = (g + norm_back(grad_n, scaled, reciprocal, gain_ref[...])).astype(BF)
    gm_ref[...] = gm
    small_ref[0:1, :] = column_sum(gm.astype(F32))
    small_ref[1:2, :] = column_sum(grad_n * scaled)
    small_ref[2:3, :] = column_sum(grad_n)
    small_ref[3:4, :] = column_sum(g)


def attn_backward_kernel(
    heads,
    step,
    out_at,
    ids_ref,
    w_ref,
    proj_ref,
    gm_ref,
    gm_sib_ref,
    wout_ref,
    gproj_ref,
    gn_own_ref,
    gn_sib_ref,
    bias_ref,
    gctx_ref,
    turned_ref,
):
    half = gm_ref.shape[0]
    width = proj_ref.shape[1] // 3
    size = width // heads
    scale = size ** (-0.5)
    core = ids_ref[1]
    mine = pl.ds(pl.multiple_of(core * width, 64), width)
    w_out = wout_ref[mine, out_at : out_at + gm_ref.shape[1]]
    for row, ref in ((0, gm_ref), (half, gm_sib_ref)):
        gctx_ref[row : row + half, :] = dot_nt(ref[...], w_out).astype(BF)
    valid = key_valid_column(ids_ref, half)
    for h in range(heads):
        at = h * size
        q_at, k_at, v_at = (slice(s * width + at, s * width + at + size) for s in range(3))
        queries, key_rows, value_rows = proj_ref[:, q_at], proj_ref[:, k_at], proj_ref[:, v_at]
        probs = head_probs(queries, key_rows, valid)
        gctx = gctx_ref[:, at : at + size]
        grad_probs = dot_nt(value_rows, gctx)
        inner = jnp.sum(probs * grad_probs, axis=0, keepdims=True)
        grad_scores = (probs * (grad_probs - inner)).astype(BF)
        turned_ref[at : at + size, :] = dot_tn(key_rows, grad_scores) * scale
        gproj_ref[:, k_at] = (dot_nn(grad_scores, queries) * scale).astype(BF)
        gproj_ref[:, v_at] = dot_nn(probs.astype(BF), gctx).astype(BF)
    gproj_ref[:, :width] = turned_ref[...].T.astype(BF)
    bias_ref[...] = column_sum(gproj_ref[...].astype(F32))
    grad_n = dot_nt(gproj_ref[...], own_columns(w_ref, step, core, 3 * width))
    gn_own_ref[...] = grad_n[:half, :]
    gn_sib_ref[...] = grad_n[half:, :].astype(BF)


def attn_weights_kernel(
    count,
    ids_ref,
    own_ref,
    sib_ref,
    gain_ref,
    shift_ref,
    ctx_ref,
    other_ref,
    gm_ref,
    gm_sib_ref,
    gproj_ref,
    *refs,
):
    kept_refs = refs[: (len(refs) - 1) // 2] if len(refs) > count + 1 else ()
    out_refs, full_ref = refs[len(kept_refs) : -1], refs[-1]
    half = own_ref.shape[0]
    width = ctx_ref.shape[1]
    core, chip = ids_ref[1], ids_ref[2]
    gm = jnp.concatenate([gm_ref[...], gm_sib_ref[...]], axis=0)
    middle = gm.shape[1] // 2
    gm_part = jnp.where(core == 0, gm[:, :middle].astype(F32), gm[:, middle:].astype(F32)).astype(BF)
    other = jnp.concatenate([other_ref[half:, :], other_ref[:half, :]], axis=0)
    mine = pl.ds(pl.multiple_of(core * width, 64), width)
    theirs = pl.ds(pl.multiple_of((1 - core) * width, 64), width)
    full_ref[mine, 3 * width :] = dot_tn(ctx_ref[...], gm_part).astype(BF)
    full_ref[theirs, 3 * width :] = dot_tn(other, gm_part).astype(BF)
    stream = jnp.concatenate([own_ref[...], sib_ref[...]], axis=0)
    scaled, _ = norm_parts(stream.astype(F32))
    normed = (scaled * gain_ref[...] + shift_ref[...]).astype(BF)
    full_ref[:, : 3 * width] = dot_tn(normed, gproj_ref[...]).astype(BF)
    if len(out_refs) == count:
        rows = full_ref.shape[0] // count
        for j, ref in enumerate(out_refs):
            if kept_refs:
                ref[rows:, :] = kept_refs[j][...]
            ref[:rows, :] = full_ref[pl.ds(pl.multiple_of((chip ^ j) * rows, 16), rows), :]
    else:
        out_refs[0][...] = full_ref[...]


def attn_norm_back_kernel(gn_ref, recv_ref, own_ref, gm_ref, gain_ref, gs_ref, small_ref):
    grad_n = gn_ref[...] + recv_ref[...].astype(F32)
    scaled, reciprocal = norm_parts(own_ref[...].astype(F32))
    term = norm_back(grad_n, scaled, reciprocal, gain_ref[...])
    gs_ref[...] = (gm_ref[...].astype(F32) + term).astype(BF)
    small_ref[0:1, :] = column_sum(grad_n * scaled)
    small_ref[1:2, :] = column_sum(grad_n)


def pack_kernel(step, count, places_ref, qkv_ref, out_ref, up_ref, *refs):
    small_refs, (mine_ref, theirs_ref, rest_ref) = refs[:8], refs[8:11]
    chip, share = places_ref[1], up_ref.shape[2] // count
    for j, ref in enumerate(refs[11:]):
        ref[:, : out_ref.shape[2]] = out_ref[0]
        at = pl.multiple_of((chip ^ j) * share, 128)
        ref[:, out_ref.shape[2] :] = up_ref[0, :, pl.ds(at, share)]
    width = out_ref.shape[2]
    cols = width // 2
    core = places_ref[0]

    def columns(l, c):
        return jnp.concatenate(
            [qkv_ref[l, :, s * width + c * cols : s * width + (c + 1) * cols] for s in range(3)],
            axis=1,
        )

    first, second = columns(0, 0).astype(F32), columns(0, 1).astype(F32)
    smalls = jnp.concatenate([ref[...].astype(F32) for ref in small_refs], axis=0).T.astype(BF)
    for flag, ref in ((core == 0, mine_ref), (core != 0, theirs_ref)):
        ref[:, : 3 * cols] = jnp.where(flag, first, second).astype(BF)
        ref[:, 3 * cols :] = smalls
    rest_ref[...] = jnp.zeros_like(rest_ref)
    for c in range(2):
        rest_ref[:, c * step : c * step + 3 * cols] = columns(1, c)
    rest_ref[:, 2 * step :] = out_ref[1]


def run(micros, kernel, outs, operands, scratch=(), smem=0):
    vmem = pl.BlockSpec(memory_space=pltpu.VMEM)
    specs = [pl.BlockSpec(memory_space=pltpu.SMEM)] * smem + [vmem] * (len(operands) - smem)
    moved = sum(o.size * o.dtype.itemsize for o in list(operands) + list(outs))
    return pl.pallas_call(
        kernel,
        out_shape=[jax.ShapeDtypeStruct(o.shape, o.dtype) for o in outs],
        in_specs=specs,
        out_specs=[vmem] * len(outs),
        scratch_shapes=[pltpu.VMEM(shape, dtype) for shape, dtype in scratch],
        cost_estimate=pl.CostEstimate(
            flops=int(micros * 1.1e9), bytes_accessed=moved, transcendentals=0
        ),
        compiler_params=pltpu.CompilerParams(vmem_limit_bytes=VMEM_LIMIT),
    )(*operands)


def like(shape, dtype):
    return jax.ShapeDtypeStruct(shape, dtype)


def swap(x, axis, bit):
    size = lax.axis_size(axis)
    return lax.ppermute(x, axis, [(i, i ^ bit) for i in range(size)])


def to_sibling(x):
    return swap(x, "dp", 1)


def swap_chip(x, j):
    return swap(x, "dp", 2 * j)


def pick(x, index):
    return lax.dynamic_index_in_dim(x, index, 0, keepdims=False)


def in_order(parts, index):
    parts, bit = list(parts), 1
    while bit < len(parts):
        flag = (index & bit) != 0
        parts = [jnp.where(flag, parts[i ^ bit], parts[i]) for i in range(len(parts))]
        bit *= 2
    return parts


def spread(x, count):
    return [x] + [swap_chip(x, j) for j in range(1, count)]


def trade(blocks, chip, count):
    return [pick(blocks, chip)] + [swap_chip(pick(blocks, chip ^ j), j) for j in range(1, count)]


def total(parts):
    return functools.reduce(lambda a, b: a + b, [p.astype(F32) for p in parts])


def section_half(x, z):
    x = x.reshape((2, 2, x.shape[0] // 4) + x.shape[1:])
    return total([pick(x, z % 2), swap(pick(x, 1 - z % 2), "section", 1)]).astype(BF)


def section_sum(half, z):
    low, high = z % 2, z // 2
    quarter = total([pick(half, high), swap(pick(half, 1 - high), "section", 2)]).astype(BF)
    half = jnp.stack(in_order([quarter, swap(quarter, "section", 2)], high))
    whole = jnp.stack(in_order([half, swap(half, "section", 1)], low))
    return whole.reshape((-1,) + whole.shape[3:])


def far_and_own(own):
    return jnp.stack([own, swap(own, "section", 2)])


def section_streams(pair, near, z, core):
    crops = in_order([pair[0], near[0], pair[1], near[1]], z)
    mine = jnp.where(core == 0, jnp.stack(crops[:2]), jnp.stack(crops[2:]))
    theirs = jnp.where(core == 0, jnp.stack(crops[2:]), jnp.stack(crops[:2]))
    recv = to_sibling(theirs)
    return jnp.concatenate(
        [jnp.where(core == 0, mine, recv), jnp.where(core == 0, recv, mine)], axis=1
    )


def after(x, *others):
    return lax.optimization_barrier((x, *others))[0]


def shards(
    residues,
    out_grad,
    key_lengths,
    masked,
    attn_gain,
    attn_shift,
    qkv_weight,
    query_bias,
    value_bias,
    out_weight,
    out_bias,
    ffn_gain,
    ffn_shift,
    up_weight,
    up_bias,
    down_weight,
    down_bias,
):
    data_count = lax.axis_size("dp")
    count = data_count // 2
    z = lax.axis_index("section")
    device = lax.axis_index("dp")
    core, chip = device % 2, device // 2
    layers, piece, triple = qkv_weight.shape
    width = triple // 3
    ff = up_weight.shape[2]
    ff_chip = ff // count
    heads = HEADS // 2
    cols = width // 2
    length = residues.shape[1]
    half = length // 2
    holder = core == z // 2
    vectors = 8
    step = -(-3 * cols // 128) * 128
    row = like((half, width), BF)

    smalls = [
        attn_gain,
        attn_shift,
        query_bias,
        value_bias,
        out_bias,
        ffn_gain,
        ffn_shift,
        down_bias,
    ]
    places = jnp.stack([core, chip]).astype(jnp.int32)
    packed = like((piece, 3 * cols + layers * vectors), BF)
    aligned = ff_chip % 128 == 0
    qkv_mine, qkv_theirs, rest1, *feed0 = run(
        2.2,
        functools.partial(pack_kernel, step, count),
        [packed, packed, like((piece, 2 * step + width), BF)]
        + [like((piece, width + ff_chip), BF)] * (count if aligned else 0),
        [places, qkv_weight, out_weight, up_weight, *smalls],
        smem=1,
    )
    if not aligned:
        feed0 = [
            jnp.concatenate(
                [out_weight[0], lax.dynamic_slice_in_dim(up_weight[0], (chip ^ j) * ff_chip, ff_chip, 1)],
                axis=1,
            )
            for j in range(count)
        ]
    pair = jnp.stack(in_order([qkv_mine, to_sibling(qkv_theirs)], core))

    residues, out_grad, key_lengths = lax.optimization_barrier(
        (residues, out_grad, key_lengths, qkv_theirs)
    )[:3]
    length_own = lax.dynamic_slice_in_dim(key_lengths, z % 2, 1, 0)
    length_here = jnp.where(holder, length_own, to_sibling(length_own))
    ids = jnp.concatenate([length_here, places])
    stream0 = pick(residues, z % 2)
    grad0 = pick(out_grad, z % 2) * pick(masked, z % 2).astype(BF)[:, None]
    stream_recv = to_sibling(stream0)
    grad_recv = to_sibling(lax.dynamic_slice_in_dim(grad0, (1 - core) * half, half, 0))
    stream0 = jnp.where(holder, stream0, stream_recv)
    g_top = jnp.where(holder, lax.dynamic_slice_in_dim(grad0, core * half, half, 0), grad_recv)
    own = lax.dynamic_slice_in_dim(stream0, core * half, half, 0)
    sib = lax.dynamic_slice_in_dim(stream0, (1 - core) * half, half, 0)

    qkv0 = jnp.stack(in_order(spread(pair, count), chip))
    qkv0 = qkv0.reshape(width, 3 * cols + layers * vectors)
    small_full = qkv0[:, 3 * cols :].T.astype(F32)
    small_full = jnp.swapaxes(small_full.reshape(vectors, layers, 1, width), 0, 1)

    def trade_up(l, dep):
        own_up = after(up_weight[l], dep)

        def block(i):
            return lax.dynamic_slice_in_dim(own_up, i * ff_chip, ff_chip, 1)

        return [block(chip)] + [swap_chip(block(chip ^ j), j) for j in range(1, count)]

    def join(parts):
        got = jnp.stack(in_order(parts, chip))
        both = jnp.stack(in_order([got, to_sibling(got)], core), axis=1)
        return both.reshape(width, -1)

    def chip_rows(own_down):
        return jnp.concatenate(in_order([own_down, to_sibling(own_down)], core), axis=0)

    feed0 = [feed0[0]] + [swap_chip(feed0[j], j) for j in range(1, count)]
    own, *feed0 = lax.optimization_barrier((own, *feed0))
    g_sent = spread(after(g_top, qkv0), count)
    upb = jnp.concatenate(in_order([up_bias, to_sibling(up_bias)], core), axis=1).astype(F32)
    zero_cols = jnp.zeros((1, cols), F32)

    def vec(l, i):
        return small_full[l, i]

    def core_bias(l):
        q = jnp.where(core == 0, vec(l, 2)[:, :cols], vec(l, 2)[:, cols:])
        v = jnp.where(core == 0, vec(l, 3)[:, :cols], vec(l, 3)[:, cols:])
        return jnp.concatenate([q, zero_cols, v], axis=1)

    qkv_full, qkv_step, out_at = [qkv0, None], [0, step], [0, 2 * step]
    up_full, down_full, out_full = [None, None], [None, None], [None, None]
    saved = []
    for l in range(layers):
        proj, ctx = run(
            6,
            functools.partial(attn_forward_kernel, heads, qkv_step[l]),
            [like((length, 3 * cols), BF), like((length, cols), BF)],
            [ids, own, sib, vec(l, 0), vec(l, 1), qkv_full[l], core_bias(l)],
            smem=1,
        )
        if l == 0:
            ctx, *g_parts = lax.optimization_barrier((ctx, *g_sent))
            out_full[0] = up_full[0] = join(feed0)
            down_full[0] = chip_rows(after(down_weight[0], own))
            rest1 = lax.all_gather(after(rest1, ctx), "dp", axis=0, tiled=True)
            qkv_full[1] = out_full[1] = rest1
        else:
            ctx, *up1 = lax.optimization_barrier((ctx, *up1))
            up_full[1] = join(up1)
            down_full[1] = chip_rows(after(down_weight[1], own))
        other = to_sibling(ctx)
        mid, normed2 = run(
            2.6,
            functools.partial(out_kernel, out_at[l]),
            [row, row],
            [ids, ctx, other, own, out_full[l], vec(l, 4), vec(l, 5), vec(l, 6)],
            smem=1,
        )
        parts = spread(normed2, count)
        saved.append((own, sib, proj, ctx, other, mid, parts))
        if l + 1 < layers:
            sums = run(
                6,
                functools.partial(ffn_forward_kernel, count),
                [row] * count,
                [*parts, up_full[l], upb[l][None], down_full[l]],
                scratch=[((count * half, width), F32)],
            )
            got = [sums[0]] + [swap_chip(sums[j], j) for j in range(1, count)]
            own = (total([mid, *got]) + vec(l, 7)).astype(BF)
            sib = to_sibling(own)
            up1 = trade_up(1, own)

    small_grads, upb_grads, ffn_grads = {}, {}, {}
    for l in reversed(range(layers)):
        own, sib, proj, ctx, other, mid, parts = saved[l]
        top = l + 1 == layers
        wide = like((count * half, ff_chip), BF)
        results = run(
            8.3,
            functools.partial(ffn_backward_kernel, count),
            [row] * count + [wide, wide, like((1, ff_chip), F32)],
            [*parts, *g_parts, up_full[l], upb[l][None], down_full[l]],
            scratch=[((count * half, width), F32)],
        )
        sums, (hidden, grad_up, upb_grads[l]) = results[:count], results[count:]
        got = [sums[0]] + [swap_chip(sums[j], j) for j in range(1, count)]
        form = like((width, ff_chip), BF)
        fw_own, fw_sib, dup, *outs = run(
            5,
            functools.partial(ffn_weights_kernel, count),
            [form, form, form] + ([row] * count if top else []),
            [ids, *parts, *g_parts, hidden, grad_up, down_full[l]],
            scratch=[((ff_chip, width), BF)],
            smem=1,
        )
        if piece % 16 != 0:
            by_core = jnp.moveaxis(dup.reshape(count, 2, piece, ff_chip), 1, 0)
            order = jnp.arange(count) ^ chip
            blocks = [
                jnp.take(pick(by_core, c), order, axis=0).reshape(cols, ff_chip)
                for c in (core, 1 - core)
            ]
            fw_own = jnp.concatenate([blocks[0], fw_own[cols:]], axis=0)
            fw_sib = jnp.concatenate([blocks[1], fw_sib[cols:]], axis=0)
        got[1] = after(got[1], fw_own)
        if not top:
            final_pair, got[1] = lax.optimization_barrier((final_pair, got[1]))
            final_near = swap(final_pair, "section", 1)
        grad_mid, small_ffn = run(
            2.3,
            functools.partial(ffn_norm_back_kernel, count),
            [row, like((4, width), F32)],
            [*got, mid, g_parts[0], vec(l, 5)],
        )
        gm_sib = to_sibling(grad_mid)
        fw_recv = to_sibling(after(fw_sib, grad_mid))
        fw_sum = total([fw_own, fw_recv]).astype(BF)
        if top:
            gm_sib, fw_sum = lax.optimization_barrier((gm_sib, fw_sum))
            ffn_grads[1] = lax.psum(fw_sum, "section")
        if top:
            outs = lax.optimization_barrier((*outs, gm_sib))[:-1]
            final_got = [outs[0]] + [swap_chip(outs[j], j) for j in range(1, count)]

        gproj, gn_own, gn_sib, gproj_sum = run(
            8,
            functools.partial(attn_backward_kernel, heads, qkv_step[l], out_at[l]),
            [like((length, 3 * cols), BF), like((half, width), F32), row, like((1, 3 * cols), F32)],
            [ids, qkv_full[l], proj, grad_mid, gm_sib, out_full[l]],
            scratch=[((length, cols), BF), ((cols, length), F32)],
            smem=1,
        )
        gn_recv = to_sibling(gn_sib)
        if top:
            gn_recv, *final_got = lax.optimization_barrier((gn_recv, *final_got))
            final_pair = far_and_own((total([mid, *final_got]) + vec(1, 7)).astype(BF))
        else:
            gn_recv, fw_sum, final_near = lax.optimization_barrier((gn_recv, fw_sum, final_near))
            final_stream = section_streams(final_pair, final_near, z, core)
            order = [list(reversed(range(lax.axis_size("section"))))]
            up_sum = lax.psum(fw_sum[:cols], "section", axis_index_groups=order)
        block_form = 2 * piece % 16 == 0
        kept = [] if top else list(packed)
        out_rows = 2 * piece if top else 4 * piece
        packed = run(
            3.8,
            functools.partial(attn_weights_kernel, count),
            [like((out_rows, 4 * cols), BF)] * count
            if block_form
            else [like((width, 4 * cols), BF)],
            [ids, own, sib, vec(l, 0), vec(l, 1), ctx, other, grad_mid, gm_sib, gproj]
            + (kept if block_form else []),
            scratch=[((width, 4 * cols), BF)],
            smem=1,
        )
        if not block_form:
            packed = packed[0].reshape(count, 2 * piece, 4 * cols)
            packed = [pick(packed, chip ^ j) for j in range(count)]
            if kept:
                packed = [jnp.concatenate([a, b], axis=0) for a, b in zip(packed, kept)]
        grad_stream, small_attn = run(
            2.2,
            attn_norm_back_kernel,
            [row, like((2, width), F32)],
            [gn_own, gn_recv, own, grad_mid, vec(l, 0)],
        )
        if top:
            g_parts = spread(grad_stream, count)
        else:
            sent = [packed[0]] + [swap_chip(packed[j], j) for j in range(1, count)]
            sent = list(lax.optimization_barrier((*sent, grad_stream))[:-1])
            pair = far_and_own(grad_stream)
            near = swap(pair, "section", 1)
            residues_grad = section_streams(pair, near, z, core).astype(F32)
            down = section_half(fw_sum[cols:], z)
            down, up_sum = lax.optimization_barrier((down, up_sum))
            down_sum = section_sum(down, z)
            packed = total(sent).astype(BF).reshape(2, 2, piece, 4 * cols)
            packed = jnp.swapaxes(packed, 0, 1)
            mine, theirs = pick(packed, core), pick(packed, 1 - core)
            both = jnp.stack(in_order([mine, to_sibling(theirs)], core), axis=1)
            both = both.reshape(4 * piece, 4 * cols)
            both = lax.psum(both, "section", axis_index_groups=[[i ^ 1 for i in range(lax.axis_size("section"))]])
            both, down_sum = lax.optimization_barrier((both, down_sum))
            attn_grads = {0: both[: 2 * piece], 1: both[2 * piece :]}
            start = after(ffn_grads[1], grad_stream)
            ffn_blocks = {
                1: (start[:cols], start[cols:]),
                0: (up_sum, down_sum),
            }
        q_sum, v_sum = gproj_sum[:, :cols], gproj_sum[:, 2 * cols :]
        spread_out = [
            jnp.where(core == 0, jnp.concatenate([s, zero_cols], 1), jnp.concatenate([zero_cols, s], 1))
            for s in (q_sum, v_sum)
        ]
        small_grads[l] = jnp.concatenate([small_attn, *spread_out, small_ffn], axis=0)

    packed = jnp.stack([small_grads[l] for l in range(layers)])
    packed = jnp.transpose(
        packed.reshape(layers, vectors, count, 2, piece), (2, 3, 0, 1, 4)
    ).reshape(count, 2, layers * vectors * piece)
    packed = total(trade(packed, chip, count))
    biases = jnp.stack([upb_grads[l] for l in range(layers)]).reshape(layers, 2, ff_chip // 2)
    biases = jnp.transpose(biases, (1, 0, 2)).reshape(2, layers * (ff_chip // 2))
    packed = jnp.concatenate([packed, biases], axis=1)
    packed = pick(packed, core) + to_sibling(pick(packed, 1 - core))
    one = packed + swap(packed, "section", 1)
    packed = one + swap(one, "section", 2)
    split = layers * vectors * piece
    grads = packed[:split].reshape(layers, vectors, piece)
    up_bias_grad = packed[split:].reshape(layers, ff_chip // 2)

    def weights(l):
        both = attn_grads[l].reshape(2, piece, 4, cols)
        qkv = jnp.transpose(both[:, :, :3], (1, 2, 0, 3)).reshape(piece, triple)
        out = jnp.transpose(both[:, :, 3], (1, 0, 2)).reshape(piece, width)
        blocks, down = ffn_blocks[l]
        blocks = [blocks[j * piece : (j + 1) * piece] for j in range(count)]
        up = in_order([blocks[0]] + [swap_chip(blocks[j], j) for j in range(1, count)], chip)
        if ff_chip >= width:
            down = [down[:, b : b + width] for b in range(0, ff_chip, width)]
            down = jnp.concatenate(down, axis=0)
        else:
            rows = ff_chip // 2
            down = [down[b : b + rows] for b in range(0, cols, rows)]
            down = jnp.concatenate(down, axis=1)
        return qkv, out, jnp.concatenate(up, axis=1), down

    per_layer = [weights(l) for l in range(layers)]
    stacked = [jnp.stack([p[i] for p in per_layer]).astype(F32) for i in range(4)]
    return (
        final_stream,
        residues_grad,
        grads[:, 0],
        grads[:, 1],
        stacked[0],
        grads[:, 2],
        grads[:, 3],
        stacked[1],
        grads[:, 4],
        grads[:, 5],
        grads[:, 6],
        stacked[2],
        up_bias_grad,
        stacked[3],
        grads[:, 7],
    )


def solution(mesh):
    rows, vector, matrix = P("dp", None, None), P(None, "dp"), P(None, "dp", None)
    weights = (
        vector,
        vector,
        matrix,
        vector,
        vector,
        matrix,
        vector,
        vector,
        vector,
        matrix,
        vector,
        matrix,
        vector,
    )
    return jax.shard_map(
        shards,
        mesh=mesh,
        in_specs=(rows, rows, P("dp"), P("dp", None), *weights),
        out_specs=(rows, rows, *weights),
        check_vma=False,
    )
```

```python
import functools

import jax
import jax.numpy as jnp
from jax import lax
from jax.experimental import pallas as pl
from jax.experimental.pallas import tpu as pltpu
from jax.sharding import PartitionSpec as P

HEADS = 20
EPSILON = 1e-05
ROOT_HALF = 0.7071067811865476
INV_ROOT_TAU = 0.3989422804014327
NEGATIVE = -1e30
BF = jnp.bfloat16
F32 = jnp.float32
VMEM_LIMIT = 24 * 1024 * 1024
VMEM_MOST = 56 * 1024 * 1024


def dot_nn(a, b):
    return jnp.dot(a, b, preferred_element_type=F32)


def dot_nt(a, b):
    return lax.dot_general(a, b, (((1,), (1,)), ((), ())), preferred_element_type=F32)


def dot_tn(a, b):
    return lax.dot_general(a, b, (((0,), (0,)), ((), ())), preferred_element_type=F32)


def norm_parts(stream):
    average = jnp.mean(stream, axis=-1, keepdims=True)
    centered = stream - average
    reciprocal = lax.rsqrt(jnp.mean(centered * centered, axis=-1, keepdims=True) + EPSILON)
    return centered * reciprocal, reciprocal


def norm_back(grad_n, scaled, reciprocal, gain):
    inner = grad_n * gain
    return reciprocal * (
        inner
        - jnp.mean(inner, axis=-1, keepdims=True)
        - scaled * jnp.mean(inner * scaled, axis=-1, keepdims=True)
    )


def own_columns(ref, step, core, width):
    if step == 0:
        return ref[:, :width]
    return ref[:, pl.ds(pl.multiple_of(core * step, 128), step)][:, :width]


def column_sum(values):
    return jnp.sum(values, axis=0, keepdims=True)


def key_valid_column(ids_ref, half):
    length, core = ids_ref[0], ids_ref[1]
    place = lax.broadcasted_iota(jnp.int32, (2 * half, 1), 0)
    own = place + core * half
    sibling = place - half + (1 - core) * half
    return jnp.where(place < half, own, sibling) < length


def head_probs(queries, key_rows, valid):
    head_size = queries.shape[1]
    scores = dot_nt(key_rows, queries) * head_size ** (-0.5)
    scores = jnp.where(valid, scores, NEGATIVE)
    exponent = jnp.exp(scores - jnp.max(scores, axis=0, keepdims=True))
    return exponent * (1.0 / jnp.sum(exponent, axis=0, keepdims=True))


def key_valid_row(ids_ref, half):
    length, core = ids_ref[0], ids_ref[1]
    place = lax.broadcasted_iota(jnp.int32, (1, 2 * half), 1)
    own = place + core * half
    sibling = place - half + (1 - core) * half
    return jnp.where(place < half, own, sibling) < length


def attn_forward_kernel(
    heads, step, ids_ref, own_ref, sib_ref, gain_ref, shift_ref, w_ref, bias_ref, *refs
):
    proj_ref, ctx_ref = refs
    half = own_ref.shape[0]
    width = ctx_ref.shape[1]
    size = width // heads
    w = own_columns(w_ref, step, ids_ref[1], 3 * width)
    for row, ref in ((0, own_ref), (half, sib_ref)):
        scaled, _ = norm_parts(ref[...].astype(F32))
        normed = (scaled * gain_ref[...] + shift_ref[...]).astype(BF)
        proj_ref[row : row + half, :] = (dot_nn(normed, w) + bias_ref[...]).astype(BF)
    valid = key_valid_row(ids_ref, half)
    for h in range(heads):
        at = h * size
        queries = proj_ref[:, at : at + size]
        key_rows = proj_ref[:, width + at : width + at + size]
        scores = dot_nt(queries, key_rows) * size ** (-0.5)
        scores = jnp.where(valid, scores, NEGATIVE)
        exponent = jnp.exp(scores - jnp.max(scores, axis=-1, keepdims=True))
        probs = exponent * (1.0 / jnp.sum(exponent, axis=-1, keepdims=True))
        ctx_ref[:, at : at + size] = dot_nn(
            probs.astype(BF), proj_ref[:, 2 * width + at : 2 * width + at + size]
        ).astype(BF)


def out_kernel(
    out_at, ids_ref, ctx_ref, other_ref, own_ref, w_ref, bias_ref, gain_ref, shift_ref, *refs
):
    mid_ref, n2_ref = refs
    half = own_ref.shape[0]
    width = ctx_ref.shape[1]
    core = ids_ref[1]
    mine = pl.ds(pl.multiple_of(core * width, 64), width)
    theirs = pl.ds(pl.multiple_of((1 - core) * width, 64), width)
    columns = slice(out_at, out_at + own_ref.shape[1])
    total = dot_nn(ctx_ref[:half, :], w_ref[mine, columns])
    total = total + dot_nn(other_ref[half:, :], w_ref[theirs, columns])
    mid = (own_ref[...].astype(F32) + total + bias_ref[...]).astype(BF)
    mid_ref[...] = mid
    scaled, _ = norm_parts(mid.astype(F32))
    n2_ref[...] = (scaled * gain_ref[...] + shift_ref[...]).astype(BF)


def ff_tiles(width):
    tile = 256 if width % 256 == 0 else width
    return [(at, tile) for at in range(0, width, tile)]


def ffn_forward_kernel(count, *refs):
    x_refs = refs[:count]
    up_ref, upb_ref, down_ref = refs[count : count + 3]
    out_refs = refs[count + 3 : 2 * count + 3]
    acc_ref = refs[-1]
    rows = x_refs[0].shape[0]
    shift = up_ref.shape[1] - upb_ref.shape[1]
    x = jnp.concatenate([ref[...] for ref in x_refs], axis=0)
    for at, tile in ff_tiles(upb_ref.shape[1]):
        up = dot_nn(x, up_ref[:, shift + at : shift + at + tile]) + upb_ref[:, at : at + tile]
        hidden = (0.5 * up * (1.0 + lax.erf(up * ROOT_HALF))).astype(BF)
        part = dot_nn(hidden, down_ref[at : at + tile, :])
        if at == 0:
            acc_ref[...] = part
        else:
            acc_ref[...] += part
    for j, ref in enumerate(out_refs):
        ref[...] = acc_ref[j * rows : (j + 1) * rows, :].astype(BF)


def ffn_backward_kernel(count, *refs):
    x_refs, g_refs = refs[:count], refs[count : 2 * count]
    up_ref, upb_ref, down_ref = refs[2 * count : 2 * count + 3]
    q_refs = refs[2 * count + 3 : 3 * count + 3]
    hidden_ref, gup_ref, dupb_ref, qacc_ref = refs[3 * count + 3 :]
    rows = x_refs[0].shape[0]
    shift = up_ref.shape[1] - upb_ref.shape[1]
    x = jnp.concatenate([ref[...] for ref in x_refs], axis=0)
    g = jnp.concatenate([ref[...] for ref in g_refs], axis=0)
    for at, tile in ff_tiles(upb_ref.shape[1]):
        up_tile = up_ref[:, shift + at : shift + at + tile]
        up = dot_nn(x, up_tile) + upb_ref[:, at : at + tile]
        bell = 0.5 * (1.0 + lax.erf(up * ROOT_HALF))
        hidden_ref[:, at : at + tile] = (up * bell).astype(BF)
        slope = bell + up * INV_ROOT_TAU * jnp.exp(-0.5 * up * up)
        grad_up = (dot_nt(g, down_ref[at : at + tile, :]) * slope).astype(BF)
        gup_ref[:, at : at + tile] = grad_up
        dupb_ref[:, at : at + tile] = column_sum(grad_up.astype(F32))
        part = dot_nt(grad_up, up_tile)
        if at == 0:
            qacc_ref[...] = part
        else:
            qacc_ref[...] += part
    for j, ref in enumerate(q_refs):
        ref[...] = qacc_ref[j * rows : (j + 1) * rows, :].astype(BF)


def ffn_weights_kernel(count, *refs):
    ids_ref, refs = refs[0], refs[1:]
    x_refs, g_refs = refs[:count], refs[count : 2 * count]
    hidden_ref, gup_ref, down_ref = refs[2 * count : 2 * count + 3]
    rest = refs[2 * count + 3 :]
    own_ref, sib_ref, dup_ref = rest[:3]
    p_refs = rest[3:-1]
    ddown_ref = rest[-1]
    rows = x_refs[0].shape[0]
    width = gup_ref.shape[1]
    core, chip = ids_ref[1], ids_ref[2]
    x = jnp.concatenate([ref[...] for ref in x_refs], axis=0)
    g = jnp.concatenate([ref[...] for ref in g_refs], axis=0)
    turned = x.T
    for at, tile in ff_tiles(width):
        ddown_ref[at : at + tile, :] = dot_tn(hidden_ref[:, at : at + tile], g).astype(BF)
        dup_ref[:, at : at + tile] = dot_nn(turned, gup_ref[:, at : at + tile]).astype(BF)
    model = x.shape[1]
    part = width // 2
    piece = model // (2 * count)
    for side, ref in ((core, own_ref), (1 - core, sib_ref)):
        for j in range(count if piece % 16 == 0 else 0):
            at = pl.multiple_of((2 * (chip ^ j) + side) * piece, 16)
            ref[j * piece : (j + 1) * piece, :] = dup_ref[pl.ds(at, piece), :]
        base = side * part
        for b in range(width // model):
            at = pl.multiple_of(base + b * (model // 2), 16)
            ref[model // 2 :, b * model : (b + 1) * model] = ddown_ref[pl.ds(at, model // 2), :]
        for b in range(model // width):
            rows_at = slice(model // 2 + b * part, model // 2 + (b + 1) * part)
            columns = slice(b * width, (b + 1) * width)
            ref[rows_at, :] = ddown_ref[pl.ds(pl.multiple_of(base, 16), part), columns]
    for j, ref in enumerate(p_refs):
        hidden = hidden_ref[j * rows : (j + 1) * rows, :]
        ref[...] = dot_nn(hidden, down_ref[...]).astype(BF)


def ffn_norm_back_kernel(count, *refs):
    q_refs = refs[:count]
    mid_ref, g_ref, gain_ref, gm_ref, small_ref = refs[count:]
    grad_n = q_refs[0][...].astype(F32)
    for ref in q_refs[1:]:
        grad_n = grad_n + ref[...].astype(F32)
    scaled, reciprocal = norm_parts(mid_ref[...].astype(F32))
    g = g_ref[...].astype(F32)
    gm = (g + norm_back(grad_n, scaled, reciprocal, gain_ref[...])).astype(BF)
    gm_ref[...] = gm
    small_ref[0:1, :] = column_sum(gm.astype(F32))
    small_ref[1:2, :] = column_sum(grad_n * scaled)
    small_ref[2:3, :] = column_sum(grad_n)
    small_ref[3:4, :] = column_sum(g)


def attn_backward_kernel(
    heads,
    step,
    out_at,
    ids_ref,
    w_ref,
    proj_ref,
    gm_ref,
    gm_sib_ref,
    wout_ref,
    gproj_ref,
    gn_own_ref,
    gn_sib_ref,
    bias_ref,
    gctx_ref,
    turned_ref,
):
    half = gm_ref.shape[0]
    width = proj_ref.shape[1] // 3
    size = width // heads
    scale = size ** (-0.5)
    core = ids_ref[1]
    mine = pl.ds(pl.multiple_of(core * width, 64), width)
    w_out = wout_ref[mine, out_at : out_at + gm_ref.shape[1]]
    for row, ref in ((0, gm_ref), (half, gm_sib_ref)):
        gctx_ref[row : row + half, :] = dot_nt(ref[...], w_out).astype(BF)
    valid = key_valid_column(ids_ref, half)
    for h in range(heads):
        at = h * size
        q_at, k_at, v_at = (slice(s * width + at, s * width + at + size) for s in range(3))
        queries, key_rows, value_rows = proj_ref[:, q_at], proj_ref[:, k_at], proj_ref[:, v_at]
        probs = head_probs(queries, key_rows, valid)
        gctx = gctx_ref[:, at : at + size]
        grad_probs = dot_nt(value_rows, gctx)
        inner = jnp.sum(probs * grad_probs, axis=0, keepdims=True)
        grad_scores = (probs * (grad_probs - inner)).astype(BF)
        turned_ref[at : at + size, :] = dot_tn(key_rows, grad_scores) * scale
        gproj_ref[:, k_at] = (dot_nn(grad_scores, queries) * scale).astype(BF)
        gproj_ref[:, v_at] = dot_nn(probs.astype(BF), gctx).astype(BF)
    gproj_ref[:, :width] = turned_ref[...].T.astype(BF)
    bias_ref[...] = column_sum(gproj_ref[...].astype(F32))
    grad_n = dot_nt(gproj_ref[...], own_columns(w_ref, step, core, 3 * width))
    gn_own_ref[...] = grad_n[:half, :]
    gn_sib_ref[...] = grad_n[half:, :].astype(BF)


def attn_weights_kernel(
    count,
    ids_ref,
    own_ref,
    sib_ref,
    gain_ref,
    shift_ref,
    ctx_ref,
    other_ref,
    gm_ref,
    gm_sib_ref,
    gproj_ref,
    *refs,
):
    kept_refs = refs[: (len(refs) - 1) // 2] if len(refs) > count + 1 else ()
    out_refs, full_ref = refs[len(kept_refs) : -1], refs[-1]
    half = own_ref.shape[0]
    width = ctx_ref.shape[1]
    core, chip = ids_ref[1], ids_ref[2]
    gm = jnp.concatenate([gm_ref[...], gm_sib_ref[...]], axis=0)
    middle = gm.shape[1] // 2
    gm_part = jnp.where(core == 0, gm[:, :middle].astype(F32), gm[:, middle:].astype(F32)).astype(BF)
    other = jnp.concatenate([other_ref[half:, :], other_ref[:half, :]], axis=0)
    mine = pl.ds(pl.multiple_of(core * width, 64), width)
    theirs = pl.ds(pl.multiple_of((1 - core) * width, 64), width)
    full_ref[mine, 3 * width :] = dot_tn(ctx_ref[...], gm_part).astype(BF)
    full_ref[theirs, 3 * width :] = dot_tn(other, gm_part).astype(BF)
    stream = jnp.concatenate([own_ref[...], sib_ref[...]], axis=0)
    scaled, _ = norm_parts(stream.astype(F32))
    normed = (scaled * gain_ref[...] + shift_ref[...]).astype(BF)
    full_ref[:, : 3 * width] = dot_tn(normed, gproj_ref[...]).astype(BF)
    if len(out_refs) == count:
        rows = full_ref.shape[0] // count
        for j, ref in enumerate(out_refs):
            if kept_refs:
                ref[rows:, :] = kept_refs[j][...]
            ref[:rows, :] = full_ref[pl.ds(pl.multiple_of((chip ^ j) * rows, 16), rows), :]
    else:
        out_refs[0][...] = full_ref[...]


def attn_norm_back_kernel(gn_ref, recv_ref, own_ref, gm_ref, gain_ref, gs_ref, small_ref):
    grad_n = gn_ref[...] + recv_ref[...].astype(F32)
    scaled, reciprocal = norm_parts(own_ref[...].astype(F32))
    term = norm_back(grad_n, scaled, reciprocal, gain_ref[...])
    gs_ref[...] = (gm_ref[...].astype(F32) + term).astype(BF)
    small_ref[0:1, :] = column_sum(grad_n * scaled)
    small_ref[1:2, :] = column_sum(grad_n)


def pack_kernel(step, count, places_ref, qkv_ref, out_ref, up_ref, *refs):
    small_refs, (mine_ref, theirs_ref, rest_ref) = refs[:8], refs[8:11]
    chip, share = places_ref[1], up_ref.shape[2] // count
    for j, ref in enumerate(refs[11:]):
        ref[:, : out_ref.shape[2]] = out_ref[0]
        at = pl.multiple_of((chip ^ j) * share, 128)
        ref[:, out_ref.shape[2] :] = up_ref[0, :, pl.ds(at, share)]
    width = out_ref.shape[2]
    cols = width // 2
    core = places_ref[0]

    def columns(l, c):
        return jnp.concatenate(
            [qkv_ref[l, :, s * width + c * cols : s * width + (c + 1) * cols] for s in range(3)],
            axis=1,
        )

    first, second = columns(0, 0).astype(F32), columns(0, 1).astype(F32)
    smalls = jnp.concatenate([ref[...].astype(F32) for ref in small_refs], axis=0).T.astype(BF)
    for flag, ref in ((core == 0, mine_ref), (core != 0, theirs_ref)):
        ref[:, : 3 * cols] = jnp.where(flag, first, second).astype(BF)
        ref[:, 3 * cols :] = smalls
    rest_ref[...] = jnp.zeros_like(rest_ref)
    for c in range(2):
        rest_ref[:, c * step : c * step + 3 * cols] = columns(1, c)
    rest_ref[:, 2 * step :] = out_ref[1]


def place_kernel(both_ref, qkv_ref, out_ref):
    layers, piece, triple = qkv_ref.shape
    width = triple // 3
    cols = width // 2
    for l in range(layers):
        for c in range(2):
            at = (2 * l + c) * piece
            part = both_ref[at : at + piece, :].astype(F32)
            for s in range(3):
                to = s * width + c * cols
                qkv_ref[l, :, to : to + cols] = part[:, s * cols : (s + 1) * cols]
            out_ref[l, :, c * cols : (c + 1) * cols] = part[:, 3 * cols :]


def run(micros, kernel, outs, operands, scratch=(), smem=0, limit=VMEM_LIMIT):
    vmem = pl.BlockSpec(memory_space=pltpu.VMEM)
    specs = [pl.BlockSpec(memory_space=pltpu.SMEM)] * smem + [vmem] * (len(operands) - smem)
    moved = sum(o.size * o.dtype.itemsize for o in list(operands) + list(outs))
    return pl.pallas_call(
        kernel,
        out_shape=[jax.ShapeDtypeStruct(o.shape, o.dtype) for o in outs],
        in_specs=specs,
        out_specs=[vmem] * len(outs),
        scratch_shapes=[pltpu.VMEM(shape, dtype) for shape, dtype in scratch],
        cost_estimate=pl.CostEstimate(
            flops=int(micros * 1.1e9), bytes_accessed=moved, transcendentals=0
        ),
        compiler_params=pltpu.CompilerParams(vmem_limit_bytes=limit),
    )(*operands)


def like(shape, dtype):
    return jax.ShapeDtypeStruct(shape, dtype)


def swap(x, axis, bit):
    size = lax.axis_size(axis)
    return lax.ppermute(x, axis, [(i, i ^ bit) for i in range(size)])


def to_sibling(x):
    return swap(x, "dp", 1)


def swap_chip(x, j):
    return swap(x, "dp", 2 * j)


def pick(x, index):
    return lax.dynamic_index_in_dim(x, index, 0, keepdims=False)


def in_order(parts, index):
    parts, bit = list(parts), 1
    while bit < len(parts):
        flag = (index & bit) != 0
        parts = [jnp.where(flag, parts[i ^ bit], parts[i]) for i in range(len(parts))]
        bit *= 2
    return parts


def spread(x, count):
    return [x] + [swap_chip(x, j) for j in range(1, count)]


def trade(blocks, chip, count):
    return [pick(blocks, chip)] + [swap_chip(pick(blocks, chip ^ j), j) for j in range(1, count)]


def total(parts):
    return functools.reduce(lambda a, b: a + b, [p.astype(F32) for p in parts])


def section_half(x, z):
    x = x.reshape((2, 2, x.shape[0] // 4) + x.shape[1:])
    return total([pick(x, z % 2), swap(pick(x, 1 - z % 2), "section", 1)]).astype(BF)


def section_sum(half, z):
    low, high = z % 2, z // 2
    quarter = total([pick(half, high), swap(pick(half, 1 - high), "section", 2)]).astype(BF)
    half = jnp.stack(in_order([quarter, swap(quarter, "section", 2)], high))
    whole = jnp.stack(in_order([half, swap(half, "section", 1)], low))
    return whole.reshape((-1,) + whole.shape[3:])


def far_and_own(own):
    return jnp.stack([own, swap(own, "section", 2)])


def section_streams(pair, near, z, core):
    crops = in_order([pair[0], near[0], pair[1], near[1]], z)
    mine = jnp.where(core == 0, jnp.stack(crops[:2]), jnp.stack(crops[2:]))
    theirs = jnp.where(core == 0, jnp.stack(crops[2:]), jnp.stack(crops[:2]))
    recv = to_sibling(theirs)
    return jnp.concatenate(
        [jnp.where(core == 0, mine, recv), jnp.where(core == 0, recv, mine)], axis=1
    )


def after(x, *others):
    return lax.optimization_barrier((x, *others))[0]


def shards(
    residues,
    out_grad,
    key_lengths,
    masked,
    attn_gain,
    attn_shift,
    qkv_weight,
    query_bias,
    value_bias,
    out_weight,
    out_bias,
    ffn_gain,
    ffn_shift,
    up_weight,
    up_bias,
    down_weight,
    down_bias,
):
    data_count = lax.axis_size("dp")
    count = data_count // 2
    z = lax.axis_index("section")
    device = lax.axis_index("dp")
    core, chip = device % 2, device // 2
    layers, piece, triple = qkv_weight.shape
    width = triple // 3
    ff = up_weight.shape[2]
    ff_chip = ff // count
    heads = HEADS // 2
    cols = width // 2
    length = residues.shape[1]
    half = length // 2
    holder = core == z // 2
    vectors = 8
    step = -(-3 * cols // 128) * 128
    row = like((half, width), BF)

    smalls = [
        attn_gain,
        attn_shift,
        query_bias,
        value_bias,
        out_bias,
        ffn_gain,
        ffn_shift,
        down_bias,
    ]
    places = jnp.stack([core, chip]).astype(jnp.int32)
    packed = like((piece, 3 * cols + layers * vectors), BF)
    aligned = ff_chip % 128 == 0
    qkv_mine, qkv_theirs, rest1, *feed0 = run(
        2.2,
        functools.partial(pack_kernel, step, count),
        [packed, packed, like((piece, 2 * step + width), BF)]
        + [like((piece, width + ff_chip), BF)] * (count if aligned else 0),
        [places, qkv_weight, out_weight, up_weight, *smalls],
        smem=1,
        limit=VMEM_MOST,
    )
    if not aligned:
        feed0 = [
            jnp.concatenate(
                [out_weight[0], lax.dynamic_slice_in_dim(up_weight[0], (chip ^ j) * ff_chip, ff_chip, 1)],
                axis=1,
            )
            for j in range(count)
        ]
    pair = jnp.stack(in_order([qkv_mine, to_sibling(qkv_theirs)], core))

    residues, out_grad, key_lengths = lax.optimization_barrier(
        (residues, out_grad, key_lengths, qkv_theirs)
    )[:3]
    length_own = lax.dynamic_slice_in_dim(key_lengths, z % 2, 1, 0)
    length_here = jnp.where(holder, length_own, to_sibling(length_own))
    ids = jnp.concatenate([length_here, places])
    stream0 = pick(residues, z % 2)
    grad0 = pick(out_grad, z % 2) * pick(masked, z % 2).astype(BF)[:, None]
    stream_recv = to_sibling(stream0)
    grad_recv = to_sibling(lax.dynamic_slice_in_dim(grad0, (1 - core) * half, half, 0))
    stream0 = jnp.where(holder, stream0, stream_recv)
    g_top = jnp.where(holder, lax.dynamic_slice_in_dim(grad0, core * half, half, 0), grad_recv)
    own = lax.dynamic_slice_in_dim(stream0, core * half, half, 0)
    sib = lax.dynamic_slice_in_dim(stream0, (1 - core) * half, half, 0)

    qkv0 = jnp.stack(in_order(spread(pair, count), chip))
    qkv0 = qkv0.reshape(width, 3 * cols + layers * vectors)
    small_full = qkv0[:, 3 * cols :].T.astype(F32)
    small_full = jnp.swapaxes(small_full.reshape(vectors, layers, 1, width), 0, 1)

    def trade_up(l, dep):
        own_up = after(up_weight[l], dep)

        def block(i):
            return lax.dynamic_slice_in_dim(own_up, i * ff_chip, ff_chip, 1)

        return [block(chip)] + [swap_chip(block(chip ^ j), j) for j in range(1, count)]

    def join(parts):
        got = jnp.stack(in_order(parts, chip))
        both = jnp.stack(in_order([got, to_sibling(got)], core), axis=1)
        return both.reshape(width, -1)

    def chip_rows(own_down):
        return jnp.concatenate(in_order([own_down, to_sibling(own_down)], core), axis=0)

    feed0 = [feed0[0]] + [swap_chip(feed0[j], j) for j in range(1, count)]
    own, *feed0 = lax.optimization_barrier((own, *feed0))
    g_sent = spread(after(g_top, qkv0), count)
    upb = jnp.concatenate(in_order([up_bias, to_sibling(up_bias)], core), axis=1).astype(F32)
    zero_cols = jnp.zeros((1, cols), F32)

    def vec(l, i):
        return small_full[l, i]

    def core_bias(l):
        q = jnp.where(core == 0, vec(l, 2)[:, :cols], vec(l, 2)[:, cols:])
        v = jnp.where(core == 0, vec(l, 3)[:, :cols], vec(l, 3)[:, cols:])
        return jnp.concatenate([q, zero_cols, v], axis=1)

    qkv_full, qkv_step, out_at = [qkv0, None], [0, step], [0, 2 * step]
    up_full, down_full, out_full = [None, None], [None, None], [None, None]
    saved = []
    for l in range(layers):
        proj, ctx = run(
            6,
            functools.partial(attn_forward_kernel, heads, qkv_step[l]),
            [like((length, 3 * cols), BF), like((length, cols), BF)],
            [ids, own, sib, vec(l, 0), vec(l, 1), qkv_full[l], core_bias(l)],
            smem=1,
        )
        if l == 0:
            ctx, *g_parts = lax.optimization_barrier((ctx, *g_sent))
            out_full[0] = up_full[0] = join(feed0)
            down_full[0] = chip_rows(after(down_weight[0], own))
            rest1 = lax.all_gather(after(rest1, own), "dp", axis=0, tiled=True)
            qkv_full[1] = out_full[1] = rest1
        else:
            ctx, *up1 = lax.optimization_barrier((ctx, *up1))
            up_full[1] = join(up1)
            down_full[1] = chip_rows(after(down_weight[1], own))
        other = to_sibling(ctx)
        mid, normed2 = run(
            2.6,
            functools.partial(out_kernel, out_at[l]),
            [row, row],
            [ids, ctx, other, own, out_full[l], vec(l, 4), vec(l, 5), vec(l, 6)],
            smem=1,
        )
        parts = spread(normed2, count)
        saved.append((own, sib, proj, ctx, other, mid, parts))
        if l + 1 < layers:
            sums = run(
                6,
                functools.partial(ffn_forward_kernel, count),
                [row] * count,
                [*parts, up_full[l], upb[l][None], down_full[l]],
                scratch=[((count * half, width), F32)],
            )
            got = [sums[0]] + [swap_chip(sums[j], j) for j in range(1, count)]
            own = (total([mid, *got]) + vec(l, 7)).astype(BF)
            sib = to_sibling(own)
            up1 = trade_up(1, own)

    small_grads, upb_grads, ffn_grads = {}, {}, {}
    for l in reversed(range(layers)):
        own, sib, proj, ctx, other, mid, parts = saved[l]
        top = l + 1 == layers
        wide = like((count * half, ff_chip), BF)
        results = run(
            8.3,
            functools.partial(ffn_backward_kernel, count),
            [row] * count + [wide, wide, like((1, ff_chip), F32)],
            [*parts, *g_parts, up_full[l], upb[l][None], down_full[l]],
            scratch=[((count * half, width), F32)],
        )
        sums, (hidden, grad_up, upb_grads[l]) = results[:count], results[count:]
        got = [sums[0]] + [swap_chip(sums[j], j) for j in range(1, count)]
        form = like((width, ff_chip), BF)
        fw_own, fw_sib, dup, *outs = run(
            5,
            functools.partial(ffn_weights_kernel, count),
            [form, form, form] + ([row] * count if top else []),
            [ids, *parts, *g_parts, hidden, grad_up, down_full[l]],
            scratch=[((ff_chip, width), BF)],
            smem=1,
        )
        if piece % 16 != 0:
            by_core = jnp.moveaxis(dup.reshape(count, 2, piece, ff_chip), 1, 0)
            order = jnp.arange(count) ^ chip
            blocks = [
                jnp.take(pick(by_core, c), order, axis=0).reshape(cols, ff_chip)
                for c in (core, 1 - core)
            ]
            fw_own = jnp.concatenate([blocks[0], fw_own[cols:]], axis=0)
            fw_sib = jnp.concatenate([blocks[1], fw_sib[cols:]], axis=0)
        got[1] = after(got[1], fw_own)
        if not top:
            final_pair, got[1] = lax.optimization_barrier((final_pair, got[1]))
            final_near = swap(final_pair, "section", 1)
        grad_mid, small_ffn = run(
            2.3,
            functools.partial(ffn_norm_back_kernel, count),
            [row, like((4, width), F32)],
            [*got, mid, g_parts[0], vec(l, 5)],
        )
        gm_sib = to_sibling(grad_mid)
        fw_recv = to_sibling(after(fw_sib, grad_mid))
        fw_sum = total([fw_own, fw_recv]).astype(BF)
        if top:
            gm_sib, fw_sum = lax.optimization_barrier((gm_sib, fw_sum))
            ffn_grads[1] = lax.psum(fw_sum, "section")
        if top:
            outs = lax.optimization_barrier((*outs, gm_sib))[:-1]
            final_got = [outs[0]] + [swap_chip(outs[j], j) for j in range(1, count)]

        gproj, gn_own, gn_sib, gproj_sum = run(
            8,
            functools.partial(attn_backward_kernel, heads, qkv_step[l], out_at[l]),
            [like((length, 3 * cols), BF), like((half, width), F32), row, like((1, 3 * cols), F32)],
            [ids, qkv_full[l], proj, grad_mid, gm_sib, out_full[l]],
            scratch=[((length, cols), BF), ((cols, length), F32)],
            smem=1,
        )
        gn_recv = to_sibling(gn_sib)
        if top:
            gn_recv, *final_got = lax.optimization_barrier((gn_recv, *final_got))
            final_pair = far_and_own((total([mid, *final_got]) + vec(1, 7)).astype(BF))
        else:
            gn_recv, fw_sum, final_near, ffn_grads[1] = lax.optimization_barrier(
                (gn_recv, fw_sum, final_near, ffn_grads[1])
            )
            final_stream = section_streams(final_pair, final_near, z, core)
            order = [list(reversed(range(lax.axis_size("section"))))]
            up_sum = lax.psum(fw_sum[:cols], "section", axis_index_groups=order)
        block_form = 2 * piece % 16 == 0
        kept = [] if top else list(packed)
        out_rows = 2 * piece if top else 4 * piece
        packed = run(
            3.8,
            functools.partial(attn_weights_kernel, count),
            [like((out_rows, 4 * cols), BF)] * count
            if block_form
            else [like((width, 4 * cols), BF)],
            [ids, own, sib, vec(l, 0), vec(l, 1), ctx, other, grad_mid, gm_sib, gproj]
            + (kept if block_form else []),
            scratch=[((width, 4 * cols), BF)],
            smem=1,
        )
        if not block_form:
            packed = packed[0].reshape(count, 2 * piece, 4 * cols)
            packed = [pick(packed, chip ^ j) for j in range(count)]
            if kept:
                packed = [jnp.concatenate([a, b], axis=0) for a, b in zip(packed, kept)]
        grad_stream, small_attn = run(
            2.2,
            attn_norm_back_kernel,
            [row, like((2, width), F32)],
            [gn_own, gn_recv, own, grad_mid, vec(l, 0)],
        )
        if top:
            g_parts = spread(grad_stream, count)
        else:
            sent = [packed[0]] + [swap_chip(packed[j], j) for j in range(1, count)]
            sent = list(lax.optimization_barrier((*sent, grad_stream))[:-1])
            pair = far_and_own(grad_stream)
            near = swap(pair, "section", 1)
            residues_grad = section_streams(pair, near, z, core).astype(F32)
            down = section_half(fw_sum[cols:], z)
            down, up_sum = lax.optimization_barrier((down, up_sum))
            down_sum = section_sum(down, z)
            packed = total(sent).astype(BF).reshape(2, 2, piece, 4 * cols)
            packed = jnp.swapaxes(packed, 0, 1)
            mine, theirs = pick(packed, core), pick(packed, 1 - core)
            both = jnp.stack(in_order([mine, to_sibling(theirs)], core), axis=1)
            both = both.reshape(4 * piece, 4 * cols)
            both = lax.psum(both, "section", axis_index_groups=[[i ^ 1 for i in range(lax.axis_size("section"))]])
            both, down_sum = lax.optimization_barrier((both, down_sum))
            attn_both = both
            start = after(ffn_grads[1], grad_stream)
            ffn_blocks = {
                1: (start[:cols], start[cols:]),
                0: (up_sum, down_sum),
            }
        q_sum, v_sum = gproj_sum[:, :cols], gproj_sum[:, 2 * cols :]
        spread_out = [
            jnp.where(core == 0, jnp.concatenate([s, zero_cols], 1), jnp.concatenate([zero_cols, s], 1))
            for s in (q_sum, v_sum)
        ]
        small_grads[l] = jnp.concatenate([small_attn, *spread_out, small_ffn], axis=0)

    packed = jnp.stack([small_grads[l] for l in range(layers)])
    packed = jnp.transpose(
        packed.reshape(layers, vectors, count, 2, piece), (2, 3, 0, 1, 4)
    ).reshape(count, 2, layers * vectors * piece)
    packed = total(trade(packed, chip, count))
    biases = jnp.stack([upb_grads[l] for l in range(layers)]).reshape(layers, 2, ff_chip // 2)
    biases = jnp.transpose(biases, (1, 0, 2)).reshape(2, layers * (ff_chip // 2))
    packed = jnp.concatenate([packed, biases], axis=1)
    packed = pick(packed, core) + to_sibling(pick(packed, 1 - core))
    one = packed + swap(packed, "section", 1)
    packed = one + swap(one, "section", 2)
    split = layers * vectors * piece
    grads = packed[:split].reshape(layers, vectors, piece)
    up_bias_grad = packed[split:].reshape(layers, ff_chip // 2)

    def weights(l):
        blocks, down = ffn_blocks[l]
        blocks = [blocks[j * piece : (j + 1) * piece] for j in range(count)]
        up = in_order([blocks[0]] + [swap_chip(blocks[j], j) for j in range(1, count)], chip)
        if ff_chip >= width:
            down = [down[:, b : b + width] for b in range(0, ff_chip, width)]
            down = jnp.concatenate(down, axis=0)
        else:
            rows = ff_chip // 2
            down = [down[b : b + rows] for b in range(0, cols, rows)]
            down = jnp.concatenate(down, axis=1)
        return jnp.concatenate(up, axis=1), down

    if piece % 16 == 0:
        qkv_grad, out_grad = run(
            1.5,
            place_kernel,
            [like((layers, piece, triple), F32), like((layers, piece, width), F32)],
            [attn_both],
        )
    else:
        rows = attn_both.reshape(layers, 2, piece, 4, cols).astype(F32)
        qkv_grad = jnp.transpose(rows[:, :, :, :3], (0, 2, 3, 1, 4)).reshape(layers, piece, triple)
        out_grad = jnp.transpose(rows[:, :, :, 3], (0, 2, 1, 3)).reshape(layers, piece, width)
    per_layer = [weights(l) for l in range(layers)]
    stacked = [jnp.stack([p[i] for p in per_layer]).astype(F32) for i in range(2)]
    return (
        final_stream,
        residues_grad,
        grads[:, 0],
        grads[:, 1],
        qkv_grad,
        grads[:, 2],
        grads[:, 3],
        out_grad,
        grads[:, 4],
        grads[:, 5],
        grads[:, 6],
        stacked[0],
        up_bias_grad,
        stacked[1],
        grads[:, 7],
    )


def solution(mesh):
    rows, vector, matrix = P("dp", None, None), P(None, "dp"), P(None, "dp", None)
    weights = (
        vector,
        vector,
        matrix,
        vector,
        vector,
        matrix,
        vector,
        vector,
        vector,
        matrix,
        vector,
        matrix,
        vector,
    )
    return jax.shard_map(
        shards,
        mesh=mesh,
        in_specs=(rows, rows, P("dp"), P("dp", None), *weights),
        out_specs=(rows, rows, *weights),
        check_vma=False,
    )
```

```python
import functools

import jax
import jax.numpy as jnp
from jax import lax
from jax.experimental import pallas as pl
from jax.experimental.pallas import tpu as pltpu
from jax.sharding import PartitionSpec as P

HEADS = 20
EPSILON = 1e-05
ROOT_HALF = 0.7071067811865476
INV_ROOT_TAU = 0.3989422804014327
NEGATIVE = -1e30
BF = jnp.bfloat16
F32 = jnp.float32
VMEM_LIMIT = 24 * 1024 * 1024
VMEM_MOST = 56 * 1024 * 1024


def dot_nn(a, b):
    return jnp.dot(a, b, preferred_element_type=F32)


def dot_nt(a, b):
    return lax.dot_general(a, b, (((1,), (1,)), ((), ())), preferred_element_type=F32)


def dot_tn(a, b):
    return lax.dot_general(a, b, (((0,), (0,)), ((), ())), preferred_element_type=F32)


def norm_parts(stream):
    average = jnp.mean(stream, axis=-1, keepdims=True)
    centered = stream - average
    reciprocal = lax.rsqrt(jnp.mean(centered * centered, axis=-1, keepdims=True) + EPSILON)
    return centered * reciprocal, reciprocal


def norm_back(grad_n, scaled, reciprocal, gain):
    inner = grad_n * gain
    return reciprocal * (
        inner
        - jnp.mean(inner, axis=-1, keepdims=True)
        - scaled * jnp.mean(inner * scaled, axis=-1, keepdims=True)
    )


def own_columns(ref, step, core, width):
    if step == 0:
        return ref[:, :width]
    return ref[:, pl.ds(pl.multiple_of(core * step, 128), step)][:, :width]


def column_sum(values):
    return jnp.sum(values, axis=0, keepdims=True)


def key_valid_column(ids_ref, half):
    length, core = ids_ref[0], ids_ref[1]
    place = lax.broadcasted_iota(jnp.int32, (2 * half, 1), 0)
    own = place + core * half
    sibling = place - half + (1 - core) * half
    return jnp.where(place < half, own, sibling) < length


def head_probs(queries, key_rows, valid):
    head_size = queries.shape[1]
    scores = dot_nt(key_rows, queries) * head_size ** (-0.5)
    scores = jnp.where(valid, scores, NEGATIVE)
    exponent = jnp.exp(scores - jnp.max(scores, axis=0, keepdims=True))
    return exponent * (1.0 / jnp.sum(exponent, axis=0, keepdims=True))


def key_valid_row(ids_ref, half):
    length, core = ids_ref[0], ids_ref[1]
    place = lax.broadcasted_iota(jnp.int32, (1, 2 * half), 1)
    own = place + core * half
    sibling = place - half + (1 - core) * half
    return jnp.where(place < half, own, sibling) < length


def attn_forward_kernel(
    heads, step, ids_ref, own_ref, sib_ref, gain_ref, shift_ref, w_ref, bias_ref, *refs
):
    proj_ref, ctx_ref = refs
    half = own_ref.shape[0]
    width = ctx_ref.shape[1]
    size = width // heads
    w = own_columns(w_ref, step, ids_ref[1], 3 * width)
    for row, ref in ((0, own_ref), (half, sib_ref)):
        scaled, _ = norm_parts(ref[...].astype(F32))
        normed = (scaled * gain_ref[...] + shift_ref[...]).astype(BF)
        proj_ref[row : row + half, :] = (dot_nn(normed, w) + bias_ref[...]).astype(BF)
    valid = key_valid_row(ids_ref, half)
    for h in range(heads):
        at = h * size
        queries = proj_ref[:, at : at + size]
        key_rows = proj_ref[:, width + at : width + at + size]
        scores = dot_nt(queries, key_rows) * size ** (-0.5)
        scores = jnp.where(valid, scores, NEGATIVE)
        exponent = jnp.exp(scores - jnp.max(scores, axis=-1, keepdims=True))
        probs = exponent * (1.0 / jnp.sum(exponent, axis=-1, keepdims=True))
        ctx_ref[:, at : at + size] = dot_nn(
            probs.astype(BF), proj_ref[:, 2 * width + at : 2 * width + at + size]
        ).astype(BF)


def out_kernel(
    out_at, ids_ref, ctx_ref, other_ref, own_ref, w_ref, bias_ref, gain_ref, shift_ref, *refs
):
    mid_ref, n2_ref = refs
    half = own_ref.shape[0]
    width = ctx_ref.shape[1]
    core = ids_ref[1]
    mine = pl.ds(pl.multiple_of(core * width, 64), width)
    theirs = pl.ds(pl.multiple_of((1 - core) * width, 64), width)
    columns = slice(out_at, out_at + own_ref.shape[1])
    total = dot_nn(ctx_ref[:half, :], w_ref[mine, columns])
    total = total + dot_nn(other_ref[half:, :], w_ref[theirs, columns])
    mid = (own_ref[...].astype(F32) + total + bias_ref[...]).astype(BF)
    mid_ref[...] = mid
    scaled, _ = norm_parts(mid.astype(F32))
    n2_ref[...] = (scaled * gain_ref[...] + shift_ref[...]).astype(BF)


def ff_tiles(width):
    tile = 256 if width % 256 == 0 else width
    return [(at, tile) for at in range(0, width, tile)]


def ffn_forward_kernel(count, *refs):
    x_refs = refs[:count]
    up_ref, upb_ref, down_ref = refs[count : count + 3]
    out_refs = refs[count + 3 : 2 * count + 3]
    acc_ref = refs[-1]
    rows = x_refs[0].shape[0]
    shift = up_ref.shape[1] - upb_ref.shape[1]
    x = jnp.concatenate([ref[...] for ref in x_refs], axis=0)
    for at, tile in ff_tiles(upb_ref.shape[1]):
        up = dot_nn(x, up_ref[:, shift + at : shift + at + tile]) + upb_ref[:, at : at + tile]
        hidden = (0.5 * up * (1.0 + lax.erf(up * ROOT_HALF))).astype(BF)
        part = dot_nn(hidden, down_ref[at : at + tile, :])
        if at == 0:
            acc_ref[...] = part
        else:
            acc_ref[...] += part
    for j, ref in enumerate(out_refs):
        ref[...] = acc_ref[j * rows : (j + 1) * rows, :].astype(BF)


def ffn_backward_kernel(count, *refs):
    x_refs, g_refs = refs[:count], refs[count : 2 * count]
    up_ref, upb_ref, down_ref = refs[2 * count : 2 * count + 3]
    q_refs = refs[2 * count + 3 : 3 * count + 3]
    hidden_ref, gup_ref, dupb_ref, qacc_ref = refs[3 * count + 3 :]
    rows = x_refs[0].shape[0]
    shift = up_ref.shape[1] - upb_ref.shape[1]
    x = jnp.concatenate([ref[...] for ref in x_refs], axis=0)
    g = jnp.concatenate([ref[...] for ref in g_refs], axis=0)
    for at, tile in ff_tiles(upb_ref.shape[1]):
        up_tile = up_ref[:, shift + at : shift + at + tile]
        up = dot_nn(x, up_tile) + upb_ref[:, at : at + tile]
        bell = 0.5 * (1.0 + lax.erf(up * ROOT_HALF))
        hidden_ref[:, at : at + tile] = (up * bell).astype(BF)
        slope = bell + up * INV_ROOT_TAU * jnp.exp(-0.5 * up * up)
        grad_up = (dot_nt(g, down_ref[at : at + tile, :]) * slope).astype(BF)
        gup_ref[:, at : at + tile] = grad_up
        dupb_ref[:, at : at + tile] = column_sum(grad_up.astype(F32))
        part = dot_nt(grad_up, up_tile)
        if at == 0:
            qacc_ref[...] = part
        else:
            qacc_ref[...] += part
    for j, ref in enumerate(q_refs):
        ref[...] = qacc_ref[j * rows : (j + 1) * rows, :].astype(BF)


def ffn_weights_kernel(count, *refs):
    ids_ref, refs = refs[0], refs[1:]
    x_refs, g_refs = refs[:count], refs[count : 2 * count]
    hidden_ref, gup_ref, down_ref = refs[2 * count : 2 * count + 3]
    rest = refs[2 * count + 3 :]
    own_ref, sib_ref, dup_ref = rest[:3]
    p_refs = rest[3:-1]
    ddown_ref = rest[-1]
    rows = x_refs[0].shape[0]
    width = gup_ref.shape[1]
    core, chip = ids_ref[1], ids_ref[2]
    x = jnp.concatenate([ref[...] for ref in x_refs], axis=0)
    g = jnp.concatenate([ref[...] for ref in g_refs], axis=0)
    turned = x.T
    for at, tile in ff_tiles(width):
        ddown_ref[at : at + tile, :] = dot_tn(hidden_ref[:, at : at + tile], g).astype(BF)
        dup_ref[:, at : at + tile] = dot_nn(turned, gup_ref[:, at : at + tile]).astype(BF)
    model = x.shape[1]
    part = width // 2
    piece = model // (2 * count)
    for side, ref in ((core, own_ref), (1 - core, sib_ref)):
        for j in range(count if piece % 16 == 0 else 0):
            at = pl.multiple_of((2 * (chip ^ j) + side) * piece, 16)
            ref[j * piece : (j + 1) * piece, :] = dup_ref[pl.ds(at, piece), :]
        base = side * part
        for b in range(width // model):
            at = pl.multiple_of(base + b * (model // 2), 16)
            ref[model // 2 :, b * model : (b + 1) * model] = ddown_ref[pl.ds(at, model // 2), :]
        for b in range(model // width):
            rows_at = slice(model // 2 + b * part, model // 2 + (b + 1) * part)
            columns = slice(b * width, (b + 1) * width)
            ref[rows_at, :] = ddown_ref[pl.ds(pl.multiple_of(base, 16), part), columns]
    for j, ref in enumerate(p_refs):
        hidden = hidden_ref[j * rows : (j + 1) * rows, :]
        ref[...] = dot_nn(hidden, down_ref[...]).astype(BF)


def ffn_norm_back_kernel(count, *refs):
    q_refs = refs[:count]
    mid_ref, g_ref, gain_ref, gm_ref, small_ref = refs[count:]
    grad_n = q_refs[0][...].astype(F32)
    for ref in q_refs[1:]:
        grad_n = grad_n + ref[...].astype(F32)
    scaled, reciprocal = norm_parts(mid_ref[...].astype(F32))
    g = g_ref[...].astype(F32)
    gm = (g + norm_back(grad_n, scaled, reciprocal, gain_ref[...])).astype(BF)
    gm_ref[...] = gm
    small_ref[0:1, :] = column_sum(gm.astype(F32))
    small_ref[1:2, :] = column_sum(grad_n * scaled)
    small_ref[2:3, :] = column_sum(grad_n)
    small_ref[3:4, :] = column_sum(g)


def attn_backward_kernel(
    heads,
    step,
    out_at,
    ids_ref,
    w_ref,
    proj_ref,
    gm_ref,
    gm_sib_ref,
    wout_ref,
    gproj_ref,
    gn_own_ref,
    gn_sib_ref,
    bias_ref,
    gctx_ref,
    turned_ref,
):
    half = gm_ref.shape[0]
    width = proj_ref.shape[1] // 3
    size = width // heads
    scale = size ** (-0.5)
    core = ids_ref[1]
    mine = pl.ds(pl.multiple_of(core * width, 64), width)
    w_out = wout_ref[mine, out_at : out_at + gm_ref.shape[1]]
    for row, ref in ((0, gm_ref), (half, gm_sib_ref)):
        gctx_ref[row : row + half, :] = dot_nt(ref[...], w_out).astype(BF)
    valid = key_valid_column(ids_ref, half)
    for h in range(heads):
        at = h * size
        q_at, k_at, v_at = (slice(s * width + at, s * width + at + size) for s in range(3))
        queries, key_rows, value_rows = proj_ref[:, q_at], proj_ref[:, k_at], proj_ref[:, v_at]
        probs = head_probs(queries, key_rows, valid)
        gctx = gctx_ref[:, at : at + size]
        grad_probs = dot_nt(value_rows, gctx)
        inner = jnp.sum(probs * grad_probs, axis=0, keepdims=True)
        grad_scores = (probs * (grad_probs - inner)).astype(BF)
        turned_ref[at : at + size, :] = dot_tn(key_rows, grad_scores) * scale
        gproj_ref[:, k_at] = (dot_nn(grad_scores, queries) * scale).astype(BF)
        gproj_ref[:, v_at] = dot_nn(probs.astype(BF), gctx).astype(BF)
    gproj_ref[:, :width] = turned_ref[...].T.astype(BF)
    bias_ref[...] = column_sum(gproj_ref[...].astype(F32))
    grad_n = dot_nt(gproj_ref[...], own_columns(w_ref, step, core, 3 * width))
    gn_own_ref[...] = grad_n[:half, :]
    gn_sib_ref[...] = grad_n[half:, :].astype(BF)


def attn_weights_kernel(
    count,
    ids_ref,
    own_ref,
    sib_ref,
    gain_ref,
    shift_ref,
    ctx_ref,
    other_ref,
    gm_ref,
    gm_sib_ref,
    gproj_ref,
    *refs,
):
    kept_refs = refs[: (len(refs) - 1) // 2] if len(refs) > count + 1 else ()
    out_refs, full_ref = refs[len(kept_refs) : -1], refs[-1]
    half = own_ref.shape[0]
    width = ctx_ref.shape[1]
    core, chip = ids_ref[1], ids_ref[2]
    gm = jnp.concatenate([gm_ref[...], gm_sib_ref[...]], axis=0)
    middle = gm.shape[1] // 2
    gm_part = jnp.where(core == 0, gm[:, :middle].astype(F32), gm[:, middle:].astype(F32)).astype(BF)
    other = jnp.concatenate([other_ref[half:, :], other_ref[:half, :]], axis=0)
    mine = pl.ds(pl.multiple_of(core * width, 64), width)
    theirs = pl.ds(pl.multiple_of((1 - core) * width, 64), width)
    full_ref[mine, 3 * width :] = dot_tn(ctx_ref[...], gm_part).astype(BF)
    full_ref[theirs, 3 * width :] = dot_tn(other, gm_part).astype(BF)
    stream = jnp.concatenate([own_ref[...], sib_ref[...]], axis=0)
    scaled, _ = norm_parts(stream.astype(F32))
    normed = (scaled * gain_ref[...] + shift_ref[...]).astype(BF)
    full_ref[:, : 3 * width] = dot_tn(normed, gproj_ref[...]).astype(BF)
    if len(out_refs) == count:
        rows = full_ref.shape[0] // count
        for j, ref in enumerate(out_refs):
            if kept_refs:
                ref[rows:, :] = kept_refs[j][...]
            ref[:rows, :] = full_ref[pl.ds(pl.multiple_of((chip ^ j) * rows, 16), rows), :]
    else:
        out_refs[0][...] = full_ref[...]


def attn_norm_back_kernel(gn_ref, recv_ref, own_ref, gm_ref, gain_ref, gs_ref, small_ref):
    grad_n = gn_ref[...] + recv_ref[...].astype(F32)
    scaled, reciprocal = norm_parts(own_ref[...].astype(F32))
    term = norm_back(grad_n, scaled, reciprocal, gain_ref[...])
    gs_ref[...] = (gm_ref[...].astype(F32) + term).astype(BF)
    small_ref[0:1, :] = column_sum(grad_n * scaled)
    small_ref[1:2, :] = column_sum(grad_n)


def pack_kernel(step, count, places_ref, qkv_ref, out_ref, up_ref, *refs):
    small_refs, (mine_ref, theirs_ref, rest_ref) = refs[:8], refs[8:11]
    chip, share = places_ref[1], up_ref.shape[2] // count
    for j, ref in enumerate(refs[11:]):
        ref[:, : out_ref.shape[2]] = out_ref[0]
        at = pl.multiple_of((chip ^ j) * share, 128)
        ref[:, out_ref.shape[2] :] = up_ref[0, :, pl.ds(at, share)]
    width = out_ref.shape[2]
    cols = width // 2
    core = places_ref[0]

    def columns(l, c):
        return jnp.concatenate(
            [qkv_ref[l, :, s * width + c * cols : s * width + (c + 1) * cols] for s in range(3)],
            axis=1,
        )

    first, second = columns(0, 0).astype(F32), columns(0, 1).astype(F32)
    smalls = jnp.concatenate([ref[...].astype(F32) for ref in small_refs], axis=0).T.astype(BF)
    for flag, ref in ((core == 0, mine_ref), (core != 0, theirs_ref)):
        ref[:, : 3 * cols] = jnp.where(flag, first, second).astype(BF)
        ref[:, 3 * cols :] = smalls
    rest_ref[...] = jnp.zeros_like(rest_ref)
    for c in range(2):
        rest_ref[:, c * step : c * step + 3 * cols] = columns(1, c)
    rest_ref[:, 2 * step :] = out_ref[1]


def place_kernel(both_ref, qkv_ref, out_ref):
    layers, piece, triple = qkv_ref.shape
    width = triple // 3
    cols = width // 2
    for l in range(layers):
        for c in range(2):
            at = (2 * l + c) * piece
            part = both_ref[at : at + piece, :].astype(F32)
            for s in range(3):
                to = s * width + c * cols
                qkv_ref[l, :, to : to + cols] = part[:, s * cols : (s + 1) * cols]
            out_ref[l, :, c * cols : (c + 1) * cols] = part[:, 3 * cols :]


def run(micros, kernel, outs, operands, scratch=(), smem=0, limit=VMEM_LIMIT):
    vmem = pl.BlockSpec(memory_space=pltpu.VMEM)
    specs = [pl.BlockSpec(memory_space=pltpu.SMEM)] * smem + [vmem] * (len(operands) - smem)
    moved = sum(o.size * o.dtype.itemsize for o in list(operands) + list(outs))
    return pl.pallas_call(
        kernel,
        out_shape=[jax.ShapeDtypeStruct(o.shape, o.dtype) for o in outs],
        in_specs=specs,
        out_specs=[vmem] * len(outs),
        scratch_shapes=[pltpu.VMEM(shape, dtype) for shape, dtype in scratch],
        cost_estimate=pl.CostEstimate(
            flops=int(micros * 1.1e9), bytes_accessed=moved, transcendentals=0
        ),
        compiler_params=pltpu.CompilerParams(vmem_limit_bytes=limit),
    )(*operands)


def like(shape, dtype):
    return jax.ShapeDtypeStruct(shape, dtype)


def swap(x, axis, bit):
    size = lax.axis_size(axis)
    return lax.ppermute(x, axis, [(i, i ^ bit) for i in range(size)])


def to_sibling(x):
    return swap(x, "dp", 1)


def swap_chip(x, j):
    return swap(x, "dp", 2 * j)


def pick(x, index):
    return lax.dynamic_index_in_dim(x, index, 0, keepdims=False)


def in_order(parts, index):
    parts, bit = list(parts), 1
    while bit < len(parts):
        flag = (index & bit) != 0
        parts = [jnp.where(flag, parts[i ^ bit], parts[i]) for i in range(len(parts))]
        bit *= 2
    return parts


def spread(x, count):
    return [x] + [swap_chip(x, j) for j in range(1, count)]


def trade(blocks, chip, count):
    return [pick(blocks, chip)] + [swap_chip(pick(blocks, chip ^ j), j) for j in range(1, count)]


def total(parts):
    return functools.reduce(lambda a, b: a + b, [p.astype(F32) for p in parts])


def section_half(x, z):
    x = x.reshape((2, 2, x.shape[0] // 4) + x.shape[1:])
    return total([pick(x, z % 2), swap(pick(x, 1 - z % 2), "section", 1)]).astype(BF)


def section_sum(half, z):
    low, high = z % 2, z // 2
    quarter = total([pick(half, high), swap(pick(half, 1 - high), "section", 2)]).astype(BF)
    half = jnp.stack(in_order([quarter, swap(quarter, "section", 2)], high))
    whole = jnp.stack(in_order([half, swap(half, "section", 1)], low))
    return whole.reshape((-1,) + whole.shape[3:])


def far_and_own(own):
    return jnp.stack([own, swap(own, "section", 2)])


def section_streams(pair, near, z, core):
    crops = in_order([pair[0], near[0], pair[1], near[1]], z)
    mine = jnp.where(core == 0, jnp.stack(crops[:2]), jnp.stack(crops[2:]))
    theirs = jnp.where(core == 0, jnp.stack(crops[2:]), jnp.stack(crops[:2]))
    recv = to_sibling(theirs)
    return jnp.concatenate(
        [jnp.where(core == 0, mine, recv), jnp.where(core == 0, recv, mine)], axis=1
    )


def after(x, *others):
    return lax.optimization_barrier((x, *others))[0]


def shards(
    residues,
    out_grad,
    key_lengths,
    masked,
    attn_gain,
    attn_shift,
    qkv_weight,
    query_bias,
    value_bias,
    out_weight,
    out_bias,
    ffn_gain,
    ffn_shift,
    up_weight,
    up_bias,
    down_weight,
    down_bias,
):
    data_count = lax.axis_size("dp")
    count = data_count // 2
    z = lax.axis_index("section")
    device = lax.axis_index("dp")
    core, chip = device % 2, device // 2
    layers, piece, triple = qkv_weight.shape
    width = triple // 3
    ff = up_weight.shape[2]
    ff_chip = ff // count
    heads = HEADS // 2
    cols = width // 2
    length = residues.shape[1]
    half = length // 2
    holder = core == z // 2
    vectors = 8
    step = -(-3 * cols // 128) * 128
    row = like((half, width), BF)

    smalls = [
        attn_gain,
        attn_shift,
        query_bias,
        value_bias,
        out_bias,
        ffn_gain,
        ffn_shift,
        down_bias,
    ]
    places = jnp.stack([core, chip]).astype(jnp.int32)
    packed = like((piece, 3 * cols + layers * vectors), BF)
    aligned = ff_chip % 128 == 0
    qkv_mine, qkv_theirs, rest1, *feed0 = run(
        2.2,
        functools.partial(pack_kernel, step, count),
        [packed, packed, like((piece, 2 * step + width), BF)]
        + [like((piece, width + ff_chip), BF)] * (count if aligned else 0),
        [places, qkv_weight, out_weight, up_weight, *smalls],
        smem=1,
        limit=VMEM_MOST,
    )
    if not aligned:
        feed0 = [
            jnp.concatenate(
                [out_weight[0], lax.dynamic_slice_in_dim(up_weight[0], (chip ^ j) * ff_chip, ff_chip, 1)],
                axis=1,
            )
            for j in range(count)
        ]
    pair = jnp.stack(in_order([qkv_mine, to_sibling(qkv_theirs)], core))

    residues, out_grad, key_lengths = lax.optimization_barrier(
        (residues, out_grad, key_lengths, qkv_theirs)
    )[:3]
    length_own = lax.dynamic_slice_in_dim(key_lengths, z % 2, 1, 0)
    length_here = jnp.where(holder, length_own, to_sibling(length_own))
    ids = jnp.concatenate([length_here, places])
    stream0 = pick(residues, z % 2)
    grad0 = pick(out_grad, z % 2) * pick(masked, z % 2).astype(BF)[:, None]
    stream_recv = to_sibling(stream0)
    grad_recv = to_sibling(lax.dynamic_slice_in_dim(grad0, (1 - core) * half, half, 0))
    stream0 = jnp.where(holder, stream0, stream_recv)
    g_top = jnp.where(holder, lax.dynamic_slice_in_dim(grad0, core * half, half, 0), grad_recv)
    own = lax.dynamic_slice_in_dim(stream0, core * half, half, 0)
    sib = lax.dynamic_slice_in_dim(stream0, (1 - core) * half, half, 0)

    qkv0 = jnp.stack(in_order(spread(pair, count), chip))
    qkv0 = qkv0.reshape(width, 3 * cols + layers * vectors)
    small_full = qkv0[:, 3 * cols :].T.astype(F32)
    small_full = jnp.swapaxes(small_full.reshape(vectors, layers, 1, width), 0, 1)

    def trade_up(l, dep):
        own_up = after(up_weight[l], dep)

        def block(i):
            return lax.dynamic_slice_in_dim(own_up, i * ff_chip, ff_chip, 1)

        return [block(chip)] + [swap_chip(block(chip ^ j), j) for j in range(1, count)]

    def join(parts):
        got = jnp.stack(in_order(parts, chip))
        both = jnp.stack(in_order([got, to_sibling(got)], core), axis=1)
        return both.reshape(width, -1)

    def chip_rows(own_down):
        return jnp.concatenate(in_order([own_down, to_sibling(own_down)], core), axis=0)

    feed0 = [feed0[0]] + [swap_chip(feed0[j], j) for j in range(1, count)]
    own, *feed0 = lax.optimization_barrier((own, *feed0))
    g_sent = spread(after(g_top, qkv0), count)
    upb = jnp.concatenate(in_order([up_bias, to_sibling(up_bias)], core), axis=1).astype(F32)
    zero_cols = jnp.zeros((1, cols), F32)

    def vec(l, i):
        return small_full[l, i]

    def core_bias(l):
        q = jnp.where(core == 0, vec(l, 2)[:, :cols], vec(l, 2)[:, cols:])
        v = jnp.where(core == 0, vec(l, 3)[:, :cols], vec(l, 3)[:, cols:])
        return jnp.concatenate([q, zero_cols, v], axis=1)

    qkv_full, qkv_step, out_at = [qkv0, None], [0, 0], [0, 0]
    up_full, down_full, out_full = [None, None], [None, None], [None, None]
    saved = []
    for l in range(layers):
        proj, ctx = run(
            6,
            functools.partial(attn_forward_kernel, heads, qkv_step[l]),
            [like((length, 3 * cols), BF), like((length, cols), BF)],
            [ids, own, sib, vec(l, 0), vec(l, 1), qkv_full[l], core_bias(l)],
            smem=1,
            limit=VMEM_MOST,
        )
        if l == 0:
            ctx, *g_parts = lax.optimization_barrier((ctx, *g_sent))
            out_full[0] = up_full[0] = join(feed0)
            down_full[0] = chip_rows(after(down_weight[0], own))
            rest1 = lax.all_gather(after(rest1, own), "dp", axis=0, tiled=True)
            qkv_full[1] = lax.dynamic_slice_in_dim(rest1, core * step, step, 1)
            out_full[1] = rest1[:, 2 * step :]
        else:
            ctx, *up1 = lax.optimization_barrier((ctx, *up1))
            up_full[1] = join(up1)
            down_full[1] = chip_rows(after(down_weight[1], own))
        other = to_sibling(ctx)
        mid, normed2 = run(
            2.6,
            functools.partial(out_kernel, out_at[l]),
            [row, row],
            [ids, ctx, other, own, out_full[l], vec(l, 4), vec(l, 5), vec(l, 6)],
            smem=1,
        )
        parts = spread(normed2, count)
        saved.append((own, sib, proj, ctx, other, mid, parts))
        if l + 1 < layers:
            sums = run(
                6,
                functools.partial(ffn_forward_kernel, count),
                [row] * count,
                [*parts, up_full[l], upb[l][None], down_full[l]],
                scratch=[((count * half, width), F32)],
            )
            got = [sums[0]] + [swap_chip(sums[j], j) for j in range(1, count)]
            got[1], qkv_full[1], out_full[1] = lax.optimization_barrier(
                (got[1], qkv_full[1], out_full[1])
            )
            own = (total([mid, *got]) + vec(l, 7)).astype(BF)
            sib = to_sibling(own)
            up1 = trade_up(1, own)

    small_grads, upb_grads, ffn_grads = {}, {}, {}
    for l in reversed(range(layers)):
        own, sib, proj, ctx, other, mid, parts = saved[l]
        top = l + 1 == layers
        wide = like((count * half, ff_chip), BF)
        results = run(
            8.3,
            functools.partial(ffn_backward_kernel, count),
            [row] * count + [wide, wide, like((1, ff_chip), F32)],
            [*parts, *g_parts, up_full[l], upb[l][None], down_full[l]],
            scratch=[((count * half, width), F32)],
        )
        sums, (hidden, grad_up, upb_grads[l]) = results[:count], results[count:]
        got = [sums[0]] + [swap_chip(sums[j], j) for j in range(1, count)]
        form = like((width, ff_chip), BF)
        fw_own, fw_sib, dup, *outs = run(
            5,
            functools.partial(ffn_weights_kernel, count),
            [form, form, form] + ([row] * count if top else []),
            [ids, *parts, *g_parts, hidden, grad_up, down_full[l]],
            scratch=[((ff_chip, width), BF)],
            smem=1,
        )
        if piece % 16 != 0:
            by_core = jnp.moveaxis(dup.reshape(count, 2, piece, ff_chip), 1, 0)
            order = jnp.arange(count) ^ chip
            blocks = [
                jnp.take(pick(by_core, c), order, axis=0).reshape(cols, ff_chip)
                for c in (core, 1 - core)
            ]
            fw_own = jnp.concatenate([blocks[0], fw_own[cols:]], axis=0)
            fw_sib = jnp.concatenate([blocks[1], fw_sib[cols:]], axis=0)
        got[1] = after(got[1], fw_own)
        if not top:
            final_pair, got[1] = lax.optimization_barrier((final_pair, got[1]))
            final_near = swap(final_pair, "section", 1)
        grad_mid, small_ffn = run(
            2.3,
            functools.partial(ffn_norm_back_kernel, count),
            [row, like((4, width), F32)],
            [*got, mid, g_parts[0], vec(l, 5)],
        )
        gm_sib = to_sibling(grad_mid)
        fw_recv = to_sibling(after(fw_sib, grad_mid))
        fw_sum = total([fw_own, fw_recv]).astype(BF)
        if top:
            gm_sib, fw_sum = lax.optimization_barrier((gm_sib, fw_sum))
            ffn_grads[1] = lax.psum(fw_sum, "section")
        if top:
            outs = lax.optimization_barrier((*outs, gm_sib))[:-1]
            final_got = [outs[0]] + [swap_chip(outs[j], j) for j in range(1, count)]

        gproj, gn_own, gn_sib, gproj_sum = run(
            8,
            functools.partial(attn_backward_kernel, heads, qkv_step[l], out_at[l]),
            [like((length, 3 * cols), BF), like((half, width), F32), row, like((1, 3 * cols), F32)],
            [ids, qkv_full[l], proj, grad_mid, gm_sib, out_full[l]],
            scratch=[((length, cols), BF), ((cols, length), F32)],
            smem=1,
            limit=VMEM_MOST,
        )
        gn_recv = to_sibling(gn_sib)
        if top:
            gn_recv, *final_got = lax.optimization_barrier((gn_recv, *final_got))
            final_pair = far_and_own((total([mid, *final_got]) + vec(1, 7)).astype(BF))
        else:
            gn_recv, fw_sum, final_near, ffn_grads[1] = lax.optimization_barrier(
                (gn_recv, fw_sum, final_near, ffn_grads[1])
            )
            final_stream = section_streams(final_pair, final_near, z, core)
            order = [list(reversed(range(lax.axis_size("section"))))]
            up_sum = lax.psum(fw_sum[:cols], "section", axis_index_groups=order)
        block_form = 2 * piece % 16 == 0
        kept = [] if top else list(packed)
        out_rows = 2 * piece if top else 4 * piece
        packed = run(
            3.8,
            functools.partial(attn_weights_kernel, count),
            [like((out_rows, 4 * cols), BF)] * count
            if block_form
            else [like((width, 4 * cols), BF)],
            [ids, own, sib, vec(l, 0), vec(l, 1), ctx, other, grad_mid, gm_sib, gproj]
            + (kept if block_form else []),
            scratch=[((width, 4 * cols), BF)],
            smem=1,
        )
        if not block_form:
            packed = packed[0].reshape(count, 2 * piece, 4 * cols)
            packed = [pick(packed, chip ^ j) for j in range(count)]
            if kept:
                packed = [jnp.concatenate([a, b], axis=0) for a, b in zip(packed, kept)]
        grad_stream, small_attn = run(
            2.2,
            attn_norm_back_kernel,
            [row, like((2, width), F32)],
            [gn_own, gn_recv, own, grad_mid, vec(l, 0)],
        )
        if top:
            g_parts = spread(grad_stream, count)
        else:
            sent = [packed[0]] + [swap_chip(packed[j], j) for j in range(1, count)]
            sent = list(lax.optimization_barrier((*sent, grad_stream))[:-1])
            pair = far_and_own(grad_stream)
            near = swap(pair, "section", 1)
            residues_grad = section_streams(pair, near, z, core).astype(F32)
            down = section_half(fw_sum[cols:], z)
            down, up_sum = lax.optimization_barrier((down, up_sum))
            down_sum = section_sum(down, z)
            packed = total(sent).astype(BF).reshape(2, 2, piece, 4 * cols)
            packed = jnp.swapaxes(packed, 0, 1)
            mine, theirs = pick(packed, core), pick(packed, 1 - core)
            both = jnp.stack(in_order([mine, to_sibling(theirs)], core), axis=1)
            both = both.reshape(4 * piece, 4 * cols)
            both = lax.psum(both, "section", axis_index_groups=[[i ^ 1 for i in range(lax.axis_size("section"))]])
            both, down_sum = lax.optimization_barrier((both, down_sum))
            attn_both = both
            start = after(ffn_grads[1], grad_stream)
            ffn_blocks = {
                1: (start[:cols], start[cols:]),
                0: (up_sum, down_sum),
            }
        q_sum, v_sum = gproj_sum[:, :cols], gproj_sum[:, 2 * cols :]
        spread_out = [
            jnp.where(core == 0, jnp.concatenate([s, zero_cols], 1), jnp.concatenate([zero_cols, s], 1))
            for s in (q_sum, v_sum)
        ]
        small_grads[l] = jnp.concatenate([small_attn, *spread_out, small_ffn], axis=0)

    packed = jnp.stack([small_grads[l] for l in range(layers)])
    packed = jnp.transpose(
        packed.reshape(layers, vectors, count, 2, piece), (2, 3, 0, 1, 4)
    ).reshape(count, 2, layers * vectors * piece)
    packed = total(trade(packed, chip, count))
    biases = jnp.stack([upb_grads[l] for l in range(layers)]).reshape(layers, 2, ff_chip // 2)
    biases = jnp.transpose(biases, (1, 0, 2)).reshape(2, layers * (ff_chip // 2))
    packed = jnp.concatenate([packed, biases], axis=1)
    packed = pick(packed, core) + to_sibling(pick(packed, 1 - core))
    one = packed + swap(packed, "section", 1)
    packed = one + swap(one, "section", 2)
    split = layers * vectors * piece
    grads = packed[:split].reshape(layers, vectors, piece)
    up_bias_grad = packed[split:].reshape(layers, ff_chip // 2)

    def weights(l):
        blocks, down = ffn_blocks[l]
        blocks = [blocks[j * piece : (j + 1) * piece] for j in range(count)]
        up = in_order([blocks[0]] + [swap_chip(blocks[j], j) for j in range(1, count)], chip)
        if ff_chip >= width:
            down = [down[:, b : b + width] for b in range(0, ff_chip, width)]
            down = jnp.concatenate(down, axis=0)
        else:
            rows = ff_chip // 2
            down = [down[b : b + rows] for b in range(0, cols, rows)]
            down = jnp.concatenate(down, axis=1)
        return jnp.concatenate(up, axis=1), down

    if piece % 16 == 0:
        qkv_grad, out_grad = run(
            1.5,
            place_kernel,
            [like((layers, piece, triple), F32), like((layers, piece, width), F32)],
            [attn_both],
        )
    else:
        rows = attn_both.reshape(layers, 2, piece, 4, cols).astype(F32)
        qkv_grad = jnp.transpose(rows[:, :, :, :3], (0, 2, 3, 1, 4)).reshape(layers, piece, triple)
        out_grad = jnp.transpose(rows[:, :, :, 3], (0, 2, 1, 3)).reshape(layers, piece, width)
    per_layer = [weights(l) for l in range(layers)]
    stacked = [jnp.stack([p[i] for p in per_layer]).astype(F32) for i in range(2)]
    return (
        final_stream,
        residues_grad,
        grads[:, 0],
        grads[:, 1],
        qkv_grad,
        grads[:, 2],
        grads[:, 3],
        out_grad,
        grads[:, 4],
        grads[:, 5],
        grads[:, 6],
        stacked[0],
        up_bias_grad,
        stacked[1],
        grads[:, 7],
    )


def solution(mesh):
    rows, vector, matrix = P("dp", None, None), P(None, "dp"), P(None, "dp", None)
    weights = (
        vector,
        vector,
        matrix,
        vector,
        vector,
        matrix,
        vector,
        vector,
        vector,
        matrix,
        vector,
        matrix,
        vector,
    )
    return jax.shard_map(
        shards,
        mesh=mesh,
        in_specs=(rows, rows, P("dp"), P("dp", None), *weights),
        out_specs=(rows, rows, *weights),
        check_vma=False,
    )
```
